32 devices in a mesh: section: 16 (over z, y, x), rows: 2 (over core).
Axes of the slice: x: 2, y: 2, z: 4, core: 2. Of those that a mesh axis runs over, the one named last changes fastest.
Arguments:
- stream: bfloat16 [16, 2, 512, 768], P('section', None, 'rows'), may hold values from -6 to 6
- segment_ids: int32 [16, 2, 512], P('section'), may hold values from 0 to 3, as said below
- ln1_gain: bfloat16 [768], replicated, may hold values from 0.25 to 1.75
- w_qkv: bfloat16 [768, 2304], replicated, may hold values from -0.3125 to 0.3125
- w_out: bfloat16 [768, 768], replicated, may hold values from -1.25 to 1.25
- ln2_gain: bfloat16 [768], replicated, may hold values from 0.25 to 1.75
- w_up: bfloat16 [768, 3072], replicated, may hold values from -0.21875 to 0.21875
- w_down: bfloat16 [3072, 768], replicated, may hold values from -0.15625 to 0.15625
- cotangent: bfloat16 [16, 2, 512, 768], P('section', None, 'rows'), may hold values from -6 to 6
Outputs:
- hidden: bfloat16 [16, 2, 512, 768], P('section', None, 'rows')
- stream_grad: float32 [16, 2, 512, 768], P('section', None, 'rows')
- ln1_gain_grad: float32 [768], P('section')
- w_qkv_grad: float32 [768, 2304], P('section')
- w_out_grad: float32 [768, 768], P('section')
- ln2_gain_grad: float32 [768], P('section')
- w_up_grad: float32 [768, 3072], P('section')
- w_down_grad: float32 [3072, 768], P('section')
The draws below stay inside these ranges and needn't reach their ends.
Inputs may be any that keep to these rules, and one draw needn't show every extreme that they name: `segment_ids`: each sequence holds four documents, ids 0 to 3 in order, starting at position 0; indices 2g and 2g+1 of section hold equal ids; no document begins at position 256.
All inputs are finite; a program needn't handle non-finite values.
Results may differ from the reference program's by a relative error of at most 0.02.
The reference program's roundings to bfloat16 on the way count: a program that leaves them out, or rounds other values in their place, can miss the bound.
Values may be sent and summed in bfloat16 or wider, within the bound.
A program may use at most 192 MiB of HBM per device.

```python
import jax
import jax.numpy as jnp
from jax import lax

D = 768
HEAD_DIM = 64
FF = 3072
TOK_DEV = 256
MB = 2
SEQ = 512
PAIRS = 8
N_SECTION = 16


def draw_segment_ids(key, part):
    key = jax.random.fold_in(key, 7)
    candidates = jnp.concatenate([jnp.arange(1, TOK_DEV, dtype=jnp.int32), jnp.arange(TOK_DEV + 1, SEQ, dtype=jnp.int32)])
    row_keys = jax.random.split(key, PAIRS * MB)
    chosen = jax.vmap(lambda row_key: jax.random.permutation(row_key, candidates)[:3])(row_keys)
    places = jnp.arange(SEQ, dtype=jnp.int32)
    starts = jnp.any(places[None, :, None] == chosen[:, None, :], axis=-1)
    ids_flat = jnp.cumsum(starts.astype(jnp.int32), axis=-1).astype(jnp.int32)
    ids_pair = ids_flat.reshape(PAIRS, MB, SEQ)
    return jnp.repeat(ids_pair, 2, axis=0)


def block_levels(stream_key, dims, shards, smallest, high):
    gain = 1.0
    for position, blocks in shards:
        heights = jax.random.uniform(jax.random.fold_in(jax.random.fold_in(stream_key, 6), position), (blocks,), jnp.float32, smallest / len(shards), high / len(shards))
        gain = gain * jnp.repeat(jnp.exp(heights), dims[position] // blocks).reshape((-1,) + (1,) * (len(dims) - 1 - position))
    return gain


def centred(rng, dims, scale, reach, shards=(), kind=jnp.bfloat16):
    array = jax.random.normal(rng, dims, jnp.float32) * scale
    if len(shards) > 0:
        array = block_levels(rng, dims, shards, -0.22, 0.18) * array
    return jnp.clip(array, min=-reach, max=reach).astype(kind)


def setup_inputs(seed: int = 0) -> dict:
    splits = jax.random.split(jax.random.key(seed), 10)
    return {
        "stream": centred(splits[0], (N_SECTION, MB, SEQ, D), 1.0, 6.0, ((0, 16), (2, 2))),
        "segment_ids": draw_segment_ids(jax.random.fold_in(splits[9], 71), 0),
        "ln1_gain": jnp.clip(1.0 + 0.15 * jax.random.normal(splits[2], (D,), jnp.float32), 0.25, 1.75).astype(jnp.bfloat16),
        "w_qkv": centred(splits[3], (D, 3 * D), (D // 2) ** -0.5, 0.3125),
        "w_out": centred(splits[4], (D, D), (D // 32) ** -0.5, 1.25),
        "ln2_gain": jnp.clip(1.0 + 0.15 * jax.random.normal(splits[5], (D,), jnp.float32), 0.25, 1.75).astype(jnp.bfloat16),
        "w_up": centred(splits[6], (D, FF), D ** -0.5, 0.21875),
        "w_down": centred(splits[7], (FF, D), (FF // 2) ** -0.5, 0.15625),
        "cotangent": centred(splits[8], (N_SECTION, MB, SEQ, D), 1.0, 6.0, ((0, 16), (2, 2))),
    }


EPSILON = 1e-05
MASKED = -1e+30
HIGHEST = lax.Precision.HIGHEST

@jax.custom_vjp
def low(v):
    return lax.optimization_barrier(v.astype(jnp.bfloat16)).astype(jnp.float32)

@jax.custom_vjp
def low_back(v):
    return v

def low_keep(v):
    return (low(v), None)

def low_pass(kept, grad):
    return (grad,)

def back_keep(v):
    return (v, None)

def back_low(kept, grad):
    return (low(grad),)
low.defvjp(low_keep, low_pass)
low_back.defvjp(back_keep, back_low)

def layer_norm(values, gain_row):
    centered = values - lax.optimization_barrier(jnp.mean(values, axis=-1, keepdims=True))
    variance = lax.optimization_barrier(jnp.mean(centered * centered, axis=-1, keepdims=True))
    return centered * lax.rsqrt(variance + EPSILON) * gain_row

def attend(queries, key_rows, value_rows, key_places, key_ids, query_ids):
    seq_len = queries.shape[0]
    block_len = min(512, seq_len)
    block_count = seq_len // block_len
    head_count = queries.shape[1] // HEAD_DIM
    score_scale = HEAD_DIM ** (-0.5)
    keys_heads = key_rows.reshape(-1, head_count, HEAD_DIM)
    values_heads = value_rows.reshape(-1, head_count, HEAD_DIM)
    query_blocks = queries.reshape(block_count, block_len, head_count, HEAD_DIM)
    place_blocks = jnp.arange(seq_len, dtype=jnp.int32).reshape(block_count, block_len)
    id_blocks = query_ids.reshape(block_count, block_len)

    def one_block(pieces):
        query_b, place_b, ids_b = pieces
        scores = low_back(jnp.einsum('qhd,khd->hqk', query_b, keys_heads, precision=HIGHEST) * score_scale)
        allowed = (key_places[None, :] <= place_b[:, None]) & (key_ids[None, :] == ids_b[:, None])
        scores = jnp.where(allowed[None], scores, MASKED)
        largest = lax.optimization_barrier(jnp.max(scores, axis=-1, keepdims=True))
        expo_vals = jnp.exp(scores - largest)
        soft_probs = low(expo_vals / lax.optimization_barrier(jnp.sum(expo_vals, axis=-1, keepdims=True)))
        mixed = jnp.einsum('hqk,khd->qhd', soft_probs, values_heads, precision=HIGHEST)
        return mixed.reshape(block_len, head_count * HEAD_DIM)
    blocks = lax.map(jax.checkpoint(one_block), (query_blocks, place_blocks, id_blocks))
    return blocks.reshape(seq_len, head_count * HEAD_DIM)

def run_pass(block_in, prev_keys, prev_values, seq_ids, weights):
    gain_one, w_qkv, w_out, gain_two, w_up, w_down = weights
    model_width = block_in.shape[1]
    seq_len = block_in.shape[0]
    normed_one = low(layer_norm(block_in, gain_one))
    projected = jnp.dot(normed_one, w_qkv, precision=HIGHEST)
    queries = low_back(low(projected[:, :model_width]))
    key_own = low_back(low(projected[:, model_width:2 * model_width]))
    value_own = low_back(low(projected[:, 2 * model_width:]))
    places = jnp.arange(seq_len, dtype=jnp.int32)
    if prev_keys is None:
        key_rows, value_rows = (key_own, value_own)
        key_places, key_ids = (places, seq_ids)
    else:
        key_rows = jnp.concatenate([prev_keys, key_own], axis=0)
        value_rows = jnp.concatenate([prev_values, value_own], axis=0)
        key_places = jnp.concatenate([places, places])
        key_ids = jnp.concatenate([seq_ids, seq_ids])
    attended = low_back(low(attend(queries, key_rows, value_rows, key_places, key_ids, seq_ids)))
    middle = block_in + low_back(jnp.dot(attended, w_out, precision=HIGHEST))
    normed_two = low(layer_norm(middle, gain_two))
    upward = low_back(jnp.dot(normed_two, w_up, precision=HIGHEST))
    hidden_act = low(jax.nn.gelu(upward, approximate=True))
    result = middle + low_back(jnp.dot(hidden_act, w_down, precision=HIGHEST))
    return (result, key_own, value_own)

def sequence_forward(pair_in, weights, id_pair):
    first_out, first_keys, first_values = run_pass(pair_in[0], None, None, id_pair[0], weights)
    second_in = low_back(low(first_out)) + pair_in[1]
    second_out, unused_keys, unused_values = run_pass(second_in, first_keys, first_values, id_pair[1], weights)
    return jnp.stack([first_out, second_out])

def regroup(values):
    shaped = values.reshape((PAIRS, 2) + values.shape[1:])
    shaped = jnp.swapaxes(shaped, 1, 2)
    return shaped.reshape((PAIRS * values.shape[1], 2) + values.shape[2:])

def ungroup(values):
    shaped = values.reshape((PAIRS, MB, 2) + values.shape[2:])
    shaped = jnp.swapaxes(shaped, 1, 2)
    return shaped.reshape((N_SECTION, MB) + values.shape[2:])

def reference(stream, segment_ids, ln1_gain, w_qkv, w_out, ln2_gain, w_up, w_down, cotangent):
    streams = regroup(stream.astype(jnp.float32))
    cotangents = regroup(cotangent.astype(jnp.float32))
    id_pairs = regroup(segment_ids)
    weights = tuple((w.astype(jnp.float32) for w in (ln1_gain, w_qkv, w_out, ln2_gain, w_up, w_down)))

    def one_sequence(totals, item):
        pair_in, id_pair, cot_pair = item

        def forward(pair_values, weight_values):
            return sequence_forward(pair_values, weight_values, id_pair)
        outputs, backward = jax.vjp(forward, pair_in, weights)
        grad_pair, grad_weights = backward(cot_pair)
        totals = jax.tree.map(jnp.add, totals, grad_weights)
        return (totals, (outputs.astype(jnp.bfloat16), grad_pair))
    zeros_init = jax.tree.map(jnp.zeros_like, weights)
    totals, (outputs, grad_pairs) = lax.scan(one_sequence, zeros_init, (streams, id_pairs, cotangents))
    return (ungroup(outputs), ungroup(grad_pairs), totals[0], totals[1], totals[2], totals[3], totals[4], totals[5])
```

```python
import functools

import jax
import jax.numpy as jnp
from jax import lax
from jax.experimental import pallas as pl
from jax.experimental.pallas import tpu as pltpu
from jax.sharding import PartitionSpec as P

HEAD = 64
PAIR = 128
EPS = 1e-05
MASKED = -1e30
F32 = jnp.float32
BF16 = jnp.bfloat16
MESH = pl.DeviceIdType.MESH
GELU_A = 0.7978845608
GELU_B = 0.044715
CHUNK = 64
VMEM_LIMIT = 63 * 1024 * 1024


def dot(a, b):
    return jnp.dot(a, b, preferred_element_type=F32)


def dot_nt(a, b):
    return lax.dot_general(a, b, (((1,), (1,)), ((), ())), preferred_element_type=F32)


def dot_tn(a, b):
    return lax.dot_general(a, b, (((0,), (0,)), ((), ())), preferred_element_type=F32)


def low(v):
    return v.astype(BF16)


def mean_of(v):
    return jnp.sum(v, axis=-1, keepdims=True) * (1.0 / v.shape[-1])


def norm_parts(v):
    centered = v - mean_of(v)
    scale = lax.rsqrt(mean_of(centered * centered) + EPS)
    return centered * scale, scale


def by_rows(rows, body):
    def step(i, carry):
        body(pl.ds(pl.multiple_of(i * CHUNK, CHUNK), CHUNK))
        return carry

    lax.fori_loop(0, rows // CHUNK, step, 0)


def place():
    r = lax.axis_index("rows")
    s = lax.axis_index("section")
    m = lax.rem(s, 2)
    return r, s, m


def aligned(value, unit=128):
    return pl.multiple_of(value, unit)


def head_masks():
    lane = lax.broadcasted_iota(jnp.int32, (1, PAIR), 1)
    first = jnp.where(lane < HEAD, 1.0, 0.0)
    return low(first), low(1.0 - first)


def fill_bias(seg_ref, m, bias, tokens, keys_first):
    length = 2 * tokens
    row = seg_ref[0, pl.ds(m, 1), :].astype(F32)
    col = jnp.broadcast_to(row, (PAIR, length)).T
    first = lax.broadcasted_iota(jnp.int32, (tokens, tokens), 0)
    second = lax.broadcasted_iota(jnp.int32, (tokens, tokens), 1)
    for i, j in ((0, 0), (1, 0), (1, 1)):
        down, across = (j, i) if keys_first else (i, j)
        same = col[down * tokens : (down + 1) * tokens, :1] == row[:, across * tokens : (across + 1) * tokens]
        if i == j:
            same = same & ((first <= second) if keys_first else (second <= first))
        bias[i + j] = jnp.where(same, 0.0, MASKED)


def forward_kernel(
    stream, cot, seg, gains, wqkv, wout, wup, wdown,
    hidden, cotx, x_o, a_o, qkv_o, o32_o, o_o, m_o, b_o, g_o, gp_o, lse_o,
    wqkv_v, wout_v, wup_v, wdown_v, e_own, e_recv, x_v, a_v, own_qkv, qkv_v, o32_v, o_tmp, o_v,
    m_v, b_v, g_v, gp_v, h_v, hid_v, lse_c, lse_v, bias,
    in_sem, out_sem, e_sem, cot_sem, hid_sem, hid_local, q_send, q_recv, o_send, o_recv,
):
    r, s, m = place()
    tokens, width = e_own.shape
    half = width // 2
    hidden_units = wup_v.shape[1]
    pairs = half // PAIR
    core = (s, 1 - r)
    relay = (s + 1 - 2 * m, r)

    loads = [
        pltpu.make_async_copy(stream.at[0, m], e_own, in_sem.at[0]),
        pltpu.make_async_copy(wqkv, wqkv_v, in_sem.at[1]),
        pltpu.make_async_copy(wout, wout_v, in_sem.at[2]),
        pltpu.make_async_copy(wup, wup_v, in_sem.at[3]),
        pltpu.make_async_copy(wdown, wdown_v, in_sem.at[4]),
    ]
    barrier = pltpu.get_barrier_semaphore()
    pl.semaphore_signal(barrier, inc=1, device_id=core, device_id_type=MESH)
    pl.semaphore_signal(barrier, inc=1, device_id=relay, device_id_type=MESH)
    for load in loads:
        load.start()
    pl.semaphore_wait(barrier, 2)

    e_copy = pltpu.make_async_remote_copy(
        stream.at[0, 1 - m], e_recv, e_sem.at[0], e_sem.at[1], device_id=relay, device_id_type=MESH)
    e_copy.start()
    cot_copy = pltpu.make_async_remote_copy(
        cot.at[0, 1 - m], cotx, cot_sem.at[0], cot_sem.at[1], device_id=relay, device_id_type=MESH)

    fill_bias(seg, m, bias, tokens, False)
    masks = head_masks()
    stores = []

    def store(src, dst):
        copy = pltpu.make_async_copy(src, dst, out_sem.at[len(stores)])
        copy.start()
        stores.append(copy)

    def attention(p):
        lane = lax.broadcasted_iota(jnp.int32, (tokens, PAIR), 1)

        def pair_step(pair, carry):
            off = aligned(pair * PAIR)
            cols = pl.ds(off, PAIR)
            for i in range(2):
                rows = slice(i * tokens, (i + 1) * tokens)
                q = qkv_v[p, 0, rows, cols]
                mixed = []
                for h in range(2):
                    q_h = q * masks[h]
                    scores, values = [], []
                    for src in range(p + 1):
                        for j in range(i + 1):
                            at = slice(j * tokens, (j + 1) * tokens)
                            scores.append(dot_nt(q_h, qkv_v[src, 1, at, cols]) + bias[i + j])
                            values.append((src, at))
                    top = functools.reduce(jnp.maximum, scores)
                    top = jnp.max(top, axis=-1, keepdims=True)
                    expo = [jnp.exp(z - top) for z in scores]
                    total = jnp.sum(functools.reduce(jnp.add, expo), axis=-1, keepdims=True)
                    share = 1.0 / total
                    out = None
                    for e, (src, at) in zip(expo, values):
                        term = dot(low(e * share), qkv_v[src, 2, at, cols])
                        out = term if out is None else out + term
                    mixed.append(out)
                    lse = top + jnp.log(total)
                    lse_c[rows, :] = jnp.where(lane == 2 * pair + h, lse, lse_c[rows, :])
                both = jnp.where(lane < HEAD, mixed[0], mixed[1])
                o32_v[p, rows, cols] = both
                o_tmp[p, pair, i] = low(both)
            mine = pl.ds(aligned(half * r + off), PAIR)
            o_v[p, :, mine] = o_tmp[p, pair, r]
            pltpu.make_async_remote_copy(
                o_tmp.at[p, pair, 1 - r], o_v.at[p, :, mine], o_send.at[p, pair], o_recv.at[p, pair],
                device_id=core, device_id_type=MESH).start()
            return carry

        lax.fori_loop(0, pairs, pair_step, 0)

    def o_copy(p, pair):
        cols = pl.ds(aligned(half * (1 - r) + PAIR * pair), PAIR)
        return pltpu.make_async_remote_copy(
            o_tmp.at[p, pair, r], o_v.at[p, :, cols], o_send.at[p, pair], o_recv.at[p, pair],
            device_id=core, device_id_type=MESH)

    gain1 = gains[0:1, :]
    gain2 = gains[1:2, :]
    lse_c[...] = jnp.zeros_like(lse_c)

    for p in range(2):
        if p == 0:
            loads[0].wait()

            @pl.when(m == 0)
            def _():
                x_v[0] = e_own[...].astype(F32)

            @pl.when(m == 1)
            def _():
                e_copy.wait_recv()
                x_v[0] = e_recv[...].astype(F32)
        else:
            @pl.when(m == 0)
            def _():
                e_copy.wait_recv()
                x_v[1] = hid_v[0].astype(F32) + e_recv[...].astype(F32)

            @pl.when(m == 1)
            def _():
                x_v[1] = hid_v[0].astype(F32) + e_own[...].astype(F32)

        def norm_one(rows):
            xh, _ = norm_parts(x_v[p, rows, :])
            a_v[p, rows, :] = low(xh * gain1)

        by_rows(tokens, norm_one)
        if p == 0:
            loads[1].wait()
        q_copies = []
        for c in range(3):
            tile = dot(a_v[p], wqkv_v[:, c * width : (c + 1) * width])
            tile = low(tile)
            if c == 0:
                tile = tile * low(jnp.full((1, 1), HEAD ** -0.5, F32))
            own_qkv[p, c] = tile
            their = pl.ds(aligned(half * (1 - r)), half)
            copy = pltpu.make_async_remote_copy(
                own_qkv.at[p, c, :, their], qkv_v.at[p, c, pl.ds(aligned(tokens * r, 16), tokens), :],
                q_send.at[p, c], q_recv.at[p, c], device_id=core, device_id_type=MESH)
            copy.start()
            q_copies.append(copy)
        for c in range(3):
            qkv_v[p, c, pl.ds(aligned(tokens * r, 16), tokens), :] = own_qkv[p, c, :, pl.ds(aligned(half * r), half)]
        store(x_v.at[p], x_o.at[p])
        store(a_v.at[p], a_o.at[p])
        for copy in q_copies:
            copy.wait_recv()
        attention(p)
        turned = lse_c[...].T
        for h in range(2 * pairs):
            lse_v[p, h] = turned[h : h + 1, :]
        store(qkv_v.at[p], qkv_o.at[p])
        store(o32_v.at[p], o32_o.at[p])
        store(lse_v.at[p], lse_o.at[p])
        if p == 0:
            loads[2].wait()
            e_copy.wait_send()
            cot_copy.start()
        for pair in range(pairs):
            o_copy(p, pair).wait_recv()
        m_v[p] = x_v[p] + dot(o_v[p], wout_v[...])

        def norm_two(rows):
            xh, _ = norm_parts(m_v[p, rows, :])
            b_v[p, rows, :] = low(xh * gain2)

        by_rows(tokens, norm_two)
        store(o_v.at[p], o_o.at[p])
        store(m_v.at[p], m_o.at[p])
        store(b_v.at[p], b_o.at[p])
        if p == 0:
            loads[3].wait()
            loads[4].wait()
        h_v[...] = m_v[p]

        def units(t, carry):
            cols = pl.ds(aligned(t * width), width)
            u = dot(b_v[p], wup_v[:, cols])
            squared = u * u
            tan = jnp.tanh(GELU_A * u * (1.0 + GELU_B * squared))
            upper = 0.5 + 0.5 * tan
            g_v[p, :, cols] = low(u * upper)
            slope = 0.5 * u * (1.0 - tan * tan) * (GELU_A + (3.0 * GELU_A * GELU_B) * squared)
            gp_v[p, :, cols] = low(upper + slope)
            h_v[...] += dot(g_v[p, :, cols], wdown_v[pl.ds(aligned(t * width), width), :])
            return carry

        lax.fori_loop(0, hidden_units // width, units, 0)
        store(g_v.at[p], g_o.at[p])
        store(gp_v.at[p], gp_o.at[p])
        hid_v[p] = low(h_v[...])

        @pl.when(m == p)
        def _():
            pltpu.make_async_copy(hid_v.at[p], hidden.at[0, m], hid_local.at[0]).start()

        @pl.when(m != p)
        def _():
            pltpu.make_async_remote_copy(
                hid_v.at[p], hidden.at[0, m], hid_sem.at[0], hid_sem.at[1],
                device_id=relay, device_id_type=MESH).start()

    pltpu.make_async_copy(hid_v.at[m], hidden.at[0, m], hid_local.at[0]).wait()
    pltpu.make_async_remote_copy(
        hid_v.at[1 - m], hidden.at[0, 1 - m], hid_sem.at[0], hid_sem.at[1],
        device_id=relay, device_id_type=MESH).wait()
    cot_copy.wait()
    for p in range(2):
        for c in range(3):
            pltpu.make_async_remote_copy(
                own_qkv.at[p, c, :, pl.ds(aligned(half * (1 - r)), half)],
                qkv_v.at[p, c, pl.ds(aligned(tokens * r, 16), tokens), :],
                q_send.at[p, c], q_recv.at[p, c], device_id=core, device_id_type=MESH).wait_send()
        for pair in range(pairs):
            o_copy(p, pair).wait_send()
    for copy in stores:
        copy.wait()


class Route:
    def __init__(self, bits, late):
        self.bits = bits
        self.late = late

    def weights(self, r):
        n = self.bits
        if self.late:
            low_unit, rest = 1, [2 ** (n + 1 - b) for b in range(2, n)]
        else:
            low_unit, rest = 2 ** (n - 2), [2 ** (n - 1 - b) for b in range(2, n)]
        return [low_unit * (2 - r), low_unit * (1 + r)] + rest

    def slot(self, s_bits, my_bits, r):
        total = 0
        for a, b, w in zip(s_bits, my_bits, self.weights(r)):
            total = total + lax.rem(a + b, 2) * w
        return total

    def partner(self, k, s, r):
        n = self.bits
        at = k + 2 if self.late else k
        if self.late and k >= n - 2:
            at = k - (n - 2)
        unit = (1 + r) if at == 0 else (2 - r) if at == 1 else 2 ** at
        return s + (1 - 2 * lax.rem(lax.div(s, jnp.int32(1) * unit), 2)) * unit


def backward_kernel(
    bits,
    cot, cotx, seg, gains, wqkv, wout, wup, wdown, x_i, a_i, qkv_i, o32_i, o_i, m_i, b_i, g_i, gp_i, lse_i,
    sgrad, gout, gqkv, gwout, gup, gdown,
    wqkv_v, wout_v, wup_v, wdown_v, m_v, o32_v, qkv_v, lse_v, b_v, g_v,
    df_v, du_v, dc_v, ds_v, do_own, do_v, dd_v, dm_v, dn_v, bias, dkv0, ds_tmp,
    sg_send_v, sg_recv_v,
    tile, send_v, own_v, stage, ph, gs, gr,
    in_sem, sg_sem, sg_local, do_sem, ds_send, ds_recv, c_send, c_recv, rs_send, rs_recv, f_send, f_recv, gain_sem,
):
    r, s, m = place()
    tokens, width = df_v.shape[1:]
    half = width // 2
    hidden_units = wup_v.shape[1]
    tiles = hidden_units // width
    pairs = half // PAIR
    sections = 2 ** bits
    rb = width // sections
    core = (s, 1 - r)
    relay = (s + 1 - 2 * m, r)
    n_in = 0

    def load(src, dst, at):
        copy = pltpu.make_async_copy(src, dst, in_sem.at[at])
        copy.start()
        return copy

    barrier = pltpu.get_barrier_semaphore()
    mates = [core]
    for b in range(bits):
        mates.append((s + (1 - 2 * lax.rem(lax.div(s, 2 ** b), 2)) * 2 ** b, r))
    for mate in mates:
        pl.semaphore_signal(barrier, inc=1, device_id=mate, device_id_type=MESH)

    own_pass = load(cot.at[0, m], df_v.at[m], 0)
    other_pass = load(cotx, df_v.at[1 - m], 1)
    ld_down = load(wdown, wdown_v, 2)
    ld_gp1 = load(gp_i.at[1], du_v.at[1], 3)
    ld_up = load(wup, wup_v, 4)
    ld_m1 = load(m_i.at[1], m_v, 5)
    ld_out = load(wout, wout_v, 6)
    ld_qkv = load(qkv_i, qkv_v, 7)
    ld_o32 = load(o32_i.at[1], o32_v, 8)
    ld_lse = load(lse_i, lse_v, 9)
    ld_wqkv = load(wqkv, wqkv_v, 10)
    ld_gp0 = load(gp_i.at[0], du_v.at[0], 12)
    ld_g = load(g_i, g_v, 13)
    ld_b = load(b_i, b_v, 14)
    fill_bias(seg, m, bias, tokens, True)
    masks = head_masks()
    gain1 = gains[0:1, :]
    gain2 = gains[1:2, :]
    gs[0] = jnp.zeros(gs.shape[1:], F32)
    pl.semaphore_wait(barrier, len(mates))

    near = Route(bits, False)
    far = Route(bits, True)
    my_bits = [lax.rem(lax.div(s, 2 ** b), 2) for b in range(bits)]
    groups = {"down": (0, tiles, near), "up": (tiles, tiles, near), "out": (2 * tiles, 1, near), "qkv": (2 * tiles + 1, 3, near)}
    order = list(groups)

    def put_tile(lhs, rhs, slot, down_at=None):
        part = width // 2
        for piece in range(2):
            tile[...] = dot_tn(lhs(piece * part, part), rhs)
            for bb in range(sections // 2):
                b = piece * (sections // 2) + bb
                sec, at = (b, slot)
                if down_at is not None:
                    sec, at = divmod(sections * down_at + b, tiles)
                s_bits = [(sec >> k) & 1 for k in range(bits)]
                rows = slice(bb * rb, (bb + 1) * rb)
                send_v[at, near.slot(s_bits, my_bits, 1 - r)] = low(tile[rows, pl.ds(aligned(half * (1 - r)), half)])
                own_v[at, near.slot(s_bits, my_bits, r)] = low(tile[rows, pl.ds(aligned(half * r), half)])

    def core_copy(c0, n, slot):
        return pltpu.make_async_remote_copy(
            send_v.at[pl.ds(slot, n)], stage.at[pl.ds(c0, n)], c_send.at[c0], c_recv.at[c0],
            device_id=core, device_id_type=MESH)

    def add_own(c0, n, slot):
        for c in range(n):
            def step(j, carry):
                stage[c0 + c, j] = low(stage[c0 + c, j].astype(F32) + own_v[slot + c, j].astype(F32))
                return carry

            lax.fori_loop(0, sections, step, 0, unroll=4)

    def rs_copy(name, k):
        c0, n, route = groups[name]
        size = sections >> (k + 1)
        g = order.index(name)
        return pltpu.make_async_remote_copy(
            stage.at[pl.ds(c0, n), pl.ds(size, size)], ph[k].at[pl.ds(c0, n)], rs_send.at[g, k], rs_recv.at[g, k],
            device_id=(route.partner(k, s, r), r), device_id_type=MESH)

    def rs_step(name, k):
        c0, n, route = groups[name]
        if k > 0:
            rs_copy(name, k - 1).wait_recv()
            size = sections >> k
            if k < bits:
                for c in range(n):
                    def step(j, carry):
                        stage[c0 + c, j] = low(stage[c0 + c, j].astype(F32) + ph[k - 1][c0 + c, j].astype(F32))
                        return carry

                    lax.fori_loop(0, size, step, 0, unroll=min(4, size))
        if k < bits:
            rs_copy(name, k).start()
        else:
            out = {"down": gdown, "up": gup, "out": gwout, "qkv": gqkv}[name]
            for c in range(n):
                total = stage[c0 + c, 0].astype(F32) + ph[bits - 1][c0 + c, 0].astype(F32)
                if name == "down":
                    out[c * rb : (c + 1) * rb, pl.ds(aligned(half * r), half)] = total
                else:
                    out[:, pl.ds(aligned(c * width + half * r), half)] = total
            for copy in final_copies(name):
                copy.start()

    def final_copies(name):
        c0, n, _ = groups[name]
        out = {"down": gdown, "up": gup, "out": gwout, "qkv": gqkv}[name]
        views = [out.at[:, pl.ds(aligned((0 if name == "down" else c) * width + half * r), half)]
                 for c in range(1 if name == "down" else n)]
        return [pltpu.make_async_remote_copy(view, view, f_send.at[c0 + c], f_recv.at[c0 + c],
                                             device_id=core, device_id_type=MESH) for c, view in enumerate(views)]

    def gain_copy(k):
        mate = mates[k]
        return pltpu.make_async_remote_copy(
            gs.at[k], gr.at[k], gain_sem.at[0, k], gain_sem.at[1, k], device_id=mate, device_id_type=MESH)

    def gain_step(k):
        if k > 0:
            gain_copy(k - 1).wait_recv()
            gs[k] = gs[k - 1] + gr[k - 1]
        if k <= bits:
            gain_copy(k).start()
        else:
            gout[...] = gs[k]

    def do_copy(p):
        return pltpu.make_async_remote_copy(
            do_own.at[:, pl.ds(aligned(half * (1 - r)), half)], do_v.at[p, pl.ds(aligned(tokens * r, 16), tokens), :],
            do_sem.at[0, p], do_sem.at[1, p], device_id=core, device_id_type=MESH)

    def ds_copy(p, pair, sending):
        at = r if sending else 1 - r
        cols = pl.ds(aligned(half * at + PAIR * pair), PAIR)
        return pltpu.make_async_remote_copy(
            ds_tmp.at[pair, :, 1 - r], ds_v.at[:, pl.ds(p * tokens, tokens), cols], ds_send.at[p, pair],
            ds_recv.at[p, pair], device_id=core, device_id_type=MESH)

    def attention_pair(p, pair):
        off = aligned(pair * PAIR)
        cols = pl.ds(off, PAIR)
        room = width // PAIR

        def acc(src, j, kv):
            a = (2 * src + j) * 2 + kv
            if a < room:
                return dn_v.at[:, a * PAIR : (a + 1) * PAIR]
            return tile.at[0:tokens, (a - room) * PAIR : (a - room + 1) * PAIR]

        for src in range(p + 1):
            for j in range(2):
                for kv in range(2):
                    acc(src, j, kv)[...] = jnp.zeros((tokens, PAIR), F32)
        for i in range(2):
            rows = slice(i * tokens, (i + 1) * tokens)
            q = qkv_v[p, 0, rows, cols]
            g = do_v[p, rows, cols]
            dq = None
            for h in range(2):
                q_h = q * masks[h]
                g_h = g * masks[h]
                lse = lse_v[p, 2 * pair + h, :, rows]
                dd = dd_v[2 * pair + h, :, rows]
                for src in range(p + 1):
                    for j in range(i + 1):
                        at = slice(j * tokens, (j + 1) * tokens)
                        key = qkv_v[src, 1, at, cols]
                        value = qkv_v[src, 2, at, cols]
                        prob = jnp.exp(dot_nt(key, q_h) + bias[i + j] - lse)
                        d_prob = dot_nt(value, g_h)
                        d_score = low(prob * (d_prob - dd))
                        acc(src, j, 0)[...] += dot(d_score, q_h)
                        acc(src, j, 1)[...] += dot(low(prob), g_h)
                        term = dot_tn(d_score, key * masks[h])
                        dq = term if dq is None else dq + term
            ds_tmp[pair, 0, i] = low(dq * (HEAD ** -0.5))
        for j in range(2):
            at = slice(j * tokens, (j + 1) * tokens)
            for kv in range(2):
                if p == 1:
                    dkv0[kv, at, cols] = acc(0, j, kv)[...]
                    ds_tmp[pair, 1 + kv, j] = low(acc(1, j, kv)[...])
                else:
                    ds_tmp[pair, 1 + kv, j] = low(acc(0, j, kv)[...] + dkv0[kv, at, cols])
        mine = pl.ds(aligned(half * r + off), PAIR)
        for c in range(3):
            ds_v[c, pl.ds(p * tokens, tokens), mine] = ds_tmp[pair, c, r]
        ds_copy(p, pair, True).start()

    def sg_own_copy():
        return pltpu.make_async_copy(dm_v, sgrad.at[0, m], sg_local.at[0])

    head_row = lax.broadcasted_iota(jnp.int32, (16, half), 0)
    head_of = lax.broadcasted_iota(jnp.int32, (16, half), 1)
    picks = low(jnp.where((head_of >= head_row * HEAD) & (head_of < (head_row + 1) * HEAD), 1.0, 0.0))

    own_pass.wait()
    other_pass.wait()

    for p in (1, 0):
        if p == 0:
            def join(rows):
                total = df_v[0, rows, :].astype(F32) + low(dm_v[rows, :]).astype(F32)
                dn_v[rows, :] = total
                df_v[0, rows, :] = low(total)

            by_rows(tokens, join)
            ld_gp0.wait()
            ld_g.wait()
            for t in range(tiles):
                put_tile(lambda at, n: g_v[:, :, t * width + at : t * width + at + n].reshape(2 * tokens, n),
                         df_v[...].reshape(2 * tokens, width), None, t)
            core_copy(0, tiles, 0).start()
        else:
            ld_down.wait()
            ld_gp1.wait()

        def units(t, carry):
            cols = pl.ds(aligned(t * width), width)
            dg = dot_nt(df_v[p], wdown_v[cols, :])
            du_v[p, :, cols] = low(dg * du_v[p, :, cols].astype(F32))
            return carry

        lax.fori_loop(0, tiles, units, 0)
        if p == 1:
            ld_up.wait()
            ld_m1.wait()
        else:
            ld_o = load(o_i, df_v, 15)
            ld_m0.wait()

            @pl.when(m == 1)
            def _():
                sg_own_copy().wait()

        db = dot_nt(du_v[p], wup_v[...])
        dm_v[...] = db

        def norm_two_back(rows):
            xh, scale = norm_parts(m_v[rows, :])
            dy = dm_v[rows, :]
            gs[0, 1:2, :] += jnp.sum(dy * xh, axis=0, keepdims=True)
            dxh = dy * gain2
            dv = scale * (dxh - mean_of(dxh) - xh * mean_of(dxh * xh))
            grad = df_v[1, rows, :].astype(F32) if p == 1 else dn_v[rows, :]
            total = grad + dv
            dm_v[rows, :] = total
            dc_v[p, rows, :] = low(total)

        by_rows(tokens, norm_two_back)
        ld_x = load(x_i.at[p], m_v, 11 + 6 * p)
        if p == 1:
            ld_out.wait()
        else:
            do_copy(1).wait_send()
        do_own[...] = low(dot_nt(dc_v[p], wout_v[...]))
        do_copy(p).start()
        do_v[p, pl.ds(aligned(tokens * r, 16), tokens), :] = do_own[:, pl.ds(aligned(half * r), half)]
        if p == 1:
            ld_qkv.wait()
            ld_lse.wait()
            ld_o32.wait()
        else:
            ld_o320.wait()
            core_copy(0, tiles, 0).wait()
            add_own(0, tiles, 0)
            rs_step("down", 0)
        do_copy(p).wait_recv()
        for i in range(2):
            rows = slice(i * tokens, (i + 1) * tokens)
            prod = do_v[p, rows, :].astype(F32) * o32_v[rows, :]
            upper = low(prod)
            rest = low(prod - upper.astype(F32))
            sums = dot_nt(picks, upper) + dot_nt(picks, rest)
            for h in range(2 * pairs):
                dd_v[h, :, rows] = sums[h : h + 1, :]
        if p == 1:
            ld_o320 = load(o32_i.at[0], o32_v, 18)

            def pair_step(pair, carry):
                attention_pair(1, pair)
                return carry

            lax.fori_loop(0, pairs, pair_step, 0)
        else:
            ld_b.wait()
            for pair in range(pairs):
                ds_copy(1, pair, True).wait_send()
            for t in range(tiles):
                put_tile(lambda at, n: b_v[:, :, at : at + n].reshape(2 * tokens, n),
                         du_v[:, :, t * width : (t + 1) * width].reshape(2 * tokens, width), t)
                core_copy(tiles + t, 1, t).start()

            ld_a = load(a_i, b_v, 16)

            def pair_step(pair, carry):
                attention_pair(0, pair)
                return carry

            lax.fori_loop(0, 1, pair_step, 0)
            for t in range(tiles):
                core_copy(tiles + t, 1, t).wait()
                add_own(tiles + t, 1, t)
            rs_step("up", 0)
            lax.fori_loop(1, pairs, pair_step, 0)
            ld_o.wait()
            put_tile(lambda at, n: df_v[:, :, at : at + n].reshape(2 * tokens, n), dc_v[...].reshape(2 * tokens, width), 0)
            core_copy(2 * tiles, 1, 0).start()
            rs_step("down", 1)
            ld_a.wait()
        for pair in range(pairs):
            ds_copy(p, pair, False).wait_recv()
        if p == 1:
            ld_wqkv.wait()
        else:
            for c in range(3):
                put_tile(lambda at, n: b_v[:, :, at : at + n].reshape(2 * tokens, n), ds_v[c], 1 + c)
                core_copy(2 * tiles + 1 + c, 1, 1 + c).start()
            core_copy(2 * tiles, 1, 0).wait()
            add_own(2 * tiles, 1, 0)
            rs_step("out", 0)
        ld_x.wait()
        for c in range(3):
            term = dot_nt(ds_v[c, p * tokens : (p + 1) * tokens, :], wqkv_v[:, c * width : (c + 1) * width])
            dn_v[...] = term if c == 0 else dn_v[...] + term
        if p == 0:
            for c in range(3):
                core_copy(2 * tiles + 1 + c, 1, 1 + c).wait()
                add_own(2 * tiles + 1 + c, 1, 1 + c)
            rs_step("qkv", 0)

        def norm_one_back(rows):
            xh, scale = norm_parts(m_v[rows, :])
            dy = dn_v[rows, :]
            gs[0, 0:1, :] += jnp.sum(dy * xh, axis=0, keepdims=True)
            dxh = dy * gain1
            dv = scale * (dxh - mean_of(dxh) - xh * mean_of(dxh * xh))
            total = dm_v[rows, :] + dv
            dm_v[rows, :] = total

        by_rows(tokens, norm_one_back)

        @pl.when(m == p)
        def _():
            sg_own_copy().start()

        @pl.when(m != p)
        def _():
            sg_send_v[...] = low(dm_v[...])
            pltpu.make_async_remote_copy(
                sg_send_v, sg_recv_v, sg_sem.at[0], sg_sem.at[1], device_id=relay, device_id_type=MESH).start()

        if p == 1:
            ld_m0 = load(m_i.at[0], m_v, 19)

    gain_step(0)
    gain_step(1)
    rs_step("up", 1)
    rs_step("down", 2)
    rs_step("out", 1)
    gain_step(2)
    rs_step("qkv", 1)
    rs_step("up", 2)
    rs_step("down", 3)
    rs_step("out", 2)
    gain_step(3)
    rs_step("qkv", 2)
    for k in range(4, bits + 1):
        rs_step("down", k)
    for k in range(3, bits + 1):
        gain_step(k + 1)
        rs_step("up", k)
        rs_step("out", k)
        rs_step("qkv", k)
    sg_copy = pltpu.make_async_remote_copy(
        sg_send_v, sg_recv_v, sg_sem.at[0], sg_sem.at[1], device_id=relay, device_id_type=MESH)
    sg_copy.wait_recv()
    dn_v[...] = sg_recv_v[...].astype(F32)
    sg_last = pltpu.make_async_copy(dn_v, sgrad.at[0, 1 - m], sg_local.at[1])
    sg_last.start()

    for name in order:
        for copy in final_copies(name):
            copy.wait()
        for k in range(bits):
            rs_copy(name, k).wait_send()
    for k in range(bits + 1):
        gain_copy(k).wait_send()
    do_copy(0).wait_send()
    for pair in range(pairs):
        ds_copy(0, pair, True).wait_send()
    sg_copy.wait_send()

    @pl.when(m == 0)
    def _():
        sg_own_copy().wait()

    sg_last.wait()


def shape(dims, dtype):
    return jax.ShapeDtypeStruct(dims, dtype)


def forward_call(stream, cot, seg, gains, weights):
    wqkv, wout, wup, wdown = weights
    _, _, tokens, width = stream.shape
    units = wup.shape[1]
    half = width // 2
    length = 2 * tokens
    pairs = half // PAIR
    saved = [
        shape((2, tokens, width), F32),
        shape((2, tokens, width), BF16),
        shape((2, 3, length, half), BF16),
        shape((2, length, half), F32),
        shape((2, tokens, width), BF16),
        shape((2, tokens, width), F32),
        shape((2, tokens, width), BF16),
        shape((2, tokens, units), BF16),
        shape((2, tokens, units), BF16),
        shape((2, 2 * pairs, 1, length), F32),
    ]
    anyspace = pl.BlockSpec(memory_space=pl.ANY)
    vmem = pl.BlockSpec(memory_space=pltpu.VMEM)
    V = pltpu.VMEM
    sem = pltpu.SemaphoreType.DMA
    return pl.pallas_call(
        forward_kernel,
        out_shape=[shape(stream.shape, BF16), shape((tokens, width), BF16)] + saved,
        in_specs=[anyspace, anyspace, vmem, vmem] + [anyspace] * 4,
        out_specs=[anyspace] * 12,
        scratch_shapes=[
            V(wqkv.shape, BF16), V(wout.shape, BF16), V(wup.shape, BF16), V(wdown.shape, BF16),
            V((tokens, width), BF16), V((tokens, width), BF16), V((2, tokens, width), F32),
            V((2, tokens, width), BF16), V((2, 3, tokens, width), BF16), V((2, 3, length, half), BF16),
            V((2, length, half), F32), V((2, pairs, 2, tokens, PAIR), BF16), V((2, tokens, width), BF16),
            V((2, tokens, width), F32), V((2, tokens, width), BF16), V((2, tokens, units), BF16),
            V((2, tokens, units), BF16), V((tokens, width), F32), V((2, tokens, width), BF16),
            V((length, PAIR), F32), V((2, 2 * pairs, 1, length), F32), V((3, tokens, tokens), F32),
            sem((5,)), sem((20,)), sem((2,)), sem((2,)), sem((2,)), sem((1,)),
            sem((2, 3)), sem((2, 3)), sem((2, pairs)), sem((2, pairs)),
        ],
        compiler_params=pltpu.CompilerParams(collective_id=0, has_side_effects=True, vmem_limit_bytes=VMEM_LIMIT),
        name="forward",
    )(stream, cot, seg, gains, wqkv, wout, wup, wdown)


def backward_call(cot, cotx, seg, gains, weights, saved, sections):
    wqkv, wout, wup, wdown = weights
    _, _, tokens, width = cot.shape
    units = wup.shape[1]
    half = width // 2
    length = 2 * tokens
    pairs = half // PAIR
    tiles = units // width
    chunks = 2 * tiles + 4
    bits = sections.bit_length() - 1
    assert 2 ** bits == sections and bits >= 2
    rb = width // sections
    anyspace = pl.BlockSpec(memory_space=pl.ANY)
    vmem = pl.BlockSpec(memory_space=pltpu.VMEM)
    V = pltpu.VMEM
    sem = pltpu.SemaphoreType.DMA

    def body(*refs):
        n_out = 18 + 6
        n_ph = n_out + 28
        fixed, ph, rest = refs[:n_ph], refs[n_ph : n_ph + bits], refs[n_ph + bits :]
        backward_kernel(bits, *fixed, ph, *rest)

    scratch = [
        V(wqkv.shape, BF16), V(wout.shape, BF16), V(wup.shape, BF16), V(wdown.shape, BF16),
        V((tokens, width), F32), V((length, half), F32),
        V((2, 3, length, half), BF16), V((2, 2 * pairs, 1, length), F32),
        V((2, tokens, width), BF16), V((2, tokens, units), BF16),
        V((2, tokens, width), BF16), V((2, tokens, units), BF16), V((2, tokens, width), BF16),
        V((3, 2 * tokens, width), BF16), V((tokens, width), BF16), V((2, length, half), BF16),
        V((2 * pairs, 1, length), F32), V((tokens, width), F32), V((tokens, width), F32),
        V((3, tokens, tokens), F32), V((2, length, half), F32),
        V((pairs, 3, 2, tokens, PAIR), BF16),
        V((tokens, width), BF16), V((tokens, width), BF16),
        V((width // 2, width), F32), V((tiles, sections, rb, half), BF16), V((tiles, sections, rb, half), BF16),
        V((chunks, sections, rb, half), BF16),
    ]
    ph = [V((chunks, sections >> (k + 1), rb, half), BF16) for k in range(bits)]
    rest = [
        V((bits + 2, 8, width), F32), V((bits + 1, 8, width), F32),
        sem((20,)), sem((2,)), sem((2,)), sem((2, 2)), sem((2, pairs)), sem((2, pairs)),
        sem((chunks,)), sem((chunks,)), sem((4, bits)), sem((4, bits)), sem((chunks,)), sem((chunks,)),
        sem((2, bits + 1)),
    ]
    return pl.pallas_call(
        body,
        out_shape=[
            shape(cot.shape, F32), shape((8, width), F32), shape((rb, 3 * width), F32), shape((rb, width), F32),
            shape((rb, units), F32), shape((tiles * rb, width), F32),
        ],
        in_specs=[anyspace, anyspace, vmem, vmem] + [anyspace] * 14,
        out_specs=[anyspace] + [vmem] * 5,
        scratch_shapes=scratch + ph + rest,
        compiler_params=pltpu.CompilerParams(collective_id=1, has_side_effects=True, vmem_limit_bytes=VMEM_LIMIT),
        name="backward",
    )(cot, cotx, seg, gains, wqkv, wout, wup, wdown, *saved)


def per_device(stream, segment_ids, ln1_gain, w_qkv, w_out, ln2_gain, w_up, w_down, cotangent):
    sections = lax.axis_size("section")
    gains = jnp.stack([ln1_gain, ln2_gain]).astype(F32)
    weights = (w_qkv, w_out, w_up, w_down)
    hidden, cotx, *saved = forward_call(stream, cotangent, segment_ids, gains, weights)
    sgrad, gout, gqkv, gwout, gup, gdown = backward_call(cotangent, cotx, segment_ids, gains, weights, saved, sections)
    rb = gqkv.shape[0]
    own = lax.dynamic_slice(gout, (0, lax.axis_index("section") * rb), (2, rb))
    return (hidden, sgrad, own[0], gqkv, gwout, own[1], gup, gdown)


def solution(mesh):
    rows = P("section", None, "rows", None)
    assert mesh.shape["rows"] == 2
    return jax.shard_map(
        per_device,
        mesh=mesh,
        in_specs=(rows, P("section", None, None), P(), P(), P(), P(), P(), P(), rows),
        out_specs=(rows, rows, P("section"), P("section", None), P("section", None), P("section"),
                   P("section", None), P("section", None)),
        check_vma=False,
    )
```

```python
import functools

import jax
import jax.numpy as jnp
from jax import lax
from jax.experimental import pallas as pl
from jax.experimental.pallas import tpu as pltpu
from jax.sharding import PartitionSpec as P

HEAD = 64
PAIR = 128
EPS = 1e-05
MASKED = -1e30
F32 = jnp.float32
BF16 = jnp.bfloat16
MESH = pl.DeviceIdType.MESH
GELU_A = 0.7978845608
GELU_B = 0.044715
CHUNK = 64
VMEM_LIMIT = 65024 * 1024


def dot(a, b):
    return jnp.dot(a, b, preferred_element_type=F32)


def dot_nt(a, b):
    return lax.dot_general(a, b, (((1,), (1,)), ((), ())), preferred_element_type=F32)


def dot_tn(a, b):
    return lax.dot_general(a, b, (((0,), (0,)), ((), ())), preferred_element_type=F32)


def low(v):
    return v.astype(BF16)


def mean_of(v):
    return jnp.sum(v, axis=-1, keepdims=True) * (1.0 / v.shape[-1])


def norm_parts(v):
    centered = v - mean_of(v)
    scale = lax.rsqrt(mean_of(centered * centered) + EPS)
    return centered * scale, scale


def by_rows(rows, body):
    def step(i, carry):
        body(pl.ds(pl.multiple_of(i * CHUNK, CHUNK), CHUNK))
        return carry

    lax.fori_loop(0, rows // CHUNK, step, 0, unroll=True)


def place():
    r = lax.axis_index("rows")
    s = lax.axis_index("section")
    m = lax.rem(s, 2)
    return r, s, m


def aligned(value, unit=128):
    return value if isinstance(value, int) else pl.multiple_of(value, unit)


def head_masks():
    lane = lax.broadcasted_iota(jnp.int32, (1, PAIR), 1)
    first = jnp.where(lane < HEAD, 1.0, 0.0)
    return low(first), low(1.0 - first)


def fill_bias(seg_ref, m, bias, tokens):
    length = 2 * tokens
    row = seg_ref[0, pl.ds(m, 1), :].astype(F32)
    col = jnp.broadcast_to(row, (PAIR, length)).T
    key_at = lax.broadcasted_iota(jnp.int32, (tokens, tokens), 0)
    query_at = lax.broadcasted_iota(jnp.int32, (tokens, tokens), 1)
    for i, j in ((0, 0), (1, 0), (1, 1)):
        seen = col[j * tokens : (j + 1) * tokens, :1] == row[:, i * tokens : (i + 1) * tokens]
        if i == j:
            seen = seen & (key_at <= query_at)
        bias[i + j] = jnp.where(seen, 0.0, MASKED)


def forward_kernel(
    stream, cot, seg, gain1_ref, gain2_ref, wqkv, wout, wup, wdown,
    hid_o, cotx, x_o, a_o, qkv_o, o32_o, o_o, m_o, b_o, g_o, gp_o, lse_o,
    wqkv_v, wout_v, wup_v, wdown_v, e_own, e_recv, x_v, a_v, own_qkv, qkv_v, o32_v, o_tmp, o_v,
    m_v, b_v, g_v, gp_v, h_v, hid_v, lse_v, bias,
    in_sem, out_sem, e_sem, cot_sem, q_send, q_recv, o_send, o_recv,
):
    r, s, m = place()
    tokens, width = e_own.shape
    half = width // 2
    hidden_units = wup_v.shape[1]
    pairs = half // PAIR
    core = (s, 1 - r)
    relay = (s + 1 - 2 * m, r)

    loads = [
        pltpu.make_async_copy(stream.at[0, m], e_own, in_sem.at[0]),
        pltpu.make_async_copy(wqkv, wqkv_v, in_sem.at[1]),
        pltpu.make_async_copy(wout, wout_v, in_sem.at[2]),
        pltpu.make_async_copy(wup, wup_v, in_sem.at[3]),
        pltpu.make_async_copy(wdown, wdown_v, in_sem.at[4]),
    ]
    barrier = pltpu.get_barrier_semaphore()
    pl.semaphore_signal(barrier, inc=1, device_id=core, device_id_type=MESH)
    pl.semaphore_signal(barrier, inc=1, device_id=relay, device_id_type=MESH)
    for load in loads:
        load.start()
    pl.semaphore_wait(barrier, 2)

    e_copy = pltpu.make_async_remote_copy(
        stream.at[0, 1 - m], e_recv, e_sem.at[0], e_sem.at[1], device_id=relay, device_id_type=MESH)
    e_copy.start()
    cot_copy = pltpu.make_async_remote_copy(
        cot.at[0, 1 - m], cotx, cot_sem.at[0], cot_sem.at[1], device_id=relay, device_id_type=MESH)

    fill_bias(seg, m, bias, tokens)
    masks = head_masks()
    stores = []

    def store(src, dst):
        copy = pltpu.make_async_copy(src, dst, out_sem.at[len(stores)])
        copy.start()
        stores.append(copy)

    def attention(p):
        lane = lax.broadcasted_iota(jnp.int32, (tokens, PAIR), 1)

        def pair_step(pair, carry):
            off = aligned(pair * PAIR)
            cols = pl.ds(off, PAIR)
            for i in range(2):
                rows = slice(i * tokens, (i + 1) * tokens)
                q = qkv_v[p, 0, rows, cols]
                mixed = []
                for h in range(2):
                    q_h = q * masks[h]
                    scores, values = [], []
                    for src in range(p + 1):
                        for j in range(i + 1):
                            at = slice(j * tokens, (j + 1) * tokens)
                            scores.append(dot_nt(qkv_v[src, 1, at, cols], q_h) + bias[i + j])
                            values.append((src, at))
                    top = jnp.max(functools.reduce(jnp.maximum, scores), axis=0, keepdims=True)
                    expo = [jnp.exp(z - top) for z in scores]
                    total = jnp.sum(functools.reduce(jnp.add, expo), axis=0, keepdims=True)
                    share = 1.0 / total
                    out = None
                    for e, (src, at) in zip(expo, values):
                        term = dot_tn(low(e * share), qkv_v[src, 2, at, cols])
                        out = term if out is None else out + term
                    mixed.append(out)
                    lse_v[p, 2 * pair + h, :, rows] = top + jnp.log(total)
                both = jnp.where(lane < HEAD, mixed[0], mixed[1])
                o32_v[p, rows, cols] = both
                o_tmp[p, pair, i] = low(both)
            mine = pl.ds(aligned(half * r + off), PAIR)
            o_v[p, :, mine] = o_tmp[p, pair, r]
            pltpu.make_async_remote_copy(
                o_tmp.at[p, pair, 1 - r], o_v.at[p, :, mine], o_send.at[p, pair], o_recv.at[p, pair],
                device_id=core, device_id_type=MESH).start()
            return carry

        for pair in range(pairs):
            pair_step(pair, 0)

    def o_copy(p, pair):
        cols = pl.ds(aligned(half * (1 - r) + PAIR * pair), PAIR)
        return pltpu.make_async_remote_copy(
            o_tmp.at[p, pair, r], o_v.at[p, :, cols], o_send.at[p, pair], o_recv.at[p, pair],
            device_id=core, device_id_type=MESH)

    gain1 = gain1_ref[...].astype(F32).reshape(1, width)
    gain2 = gain2_ref[...].astype(F32).reshape(1, width)

    for p in range(2):
        if p == 0:
            loads[0].wait()

            @pl.when(m == 0)
            def _():
                x_v[0] = e_own[...].astype(F32)

            @pl.when(m == 1)
            def _():
                e_copy.wait_recv()
                x_v[0] = e_recv[...].astype(F32)
        else:
            @pl.when(m == 0)
            def _():
                e_copy.wait_recv()
                x_v[1] = hid_v[0].astype(F32) + e_recv[...].astype(F32)

            @pl.when(m == 1)
            def _():
                x_v[1] = hid_v[0].astype(F32) + e_own[...].astype(F32)

        def norm_one(rows):
            xh, _ = norm_parts(x_v[p, rows, :])
            a_v[p, rows, :] = low(xh * gain1)

        by_rows(tokens, norm_one)
        if p == 0:
            loads[1].wait()
        q_copies = []
        for c in range(3):
            tile = dot(a_v[p], wqkv_v[:, c * width : (c + 1) * width])
            tile = low(tile)
            if c == 0:
                tile = tile * low(jnp.full((1, 1), HEAD ** -0.5, F32))
            own_qkv[p, c] = tile
            their = pl.ds(aligned(half * (1 - r)), half)
            copy = pltpu.make_async_remote_copy(
                own_qkv.at[p, c, :, their], qkv_v.at[p, c, pl.ds(aligned(tokens * r, 16), tokens), :],
                q_send.at[p, c], q_recv.at[p, c], device_id=core, device_id_type=MESH)
            copy.start()
            q_copies.append(copy)
        for c in range(3):
            qkv_v[p, c, pl.ds(aligned(tokens * r, 16), tokens), :] = own_qkv[p, c, :, pl.ds(aligned(half * r), half)]
        store(x_v.at[p], x_o.at[p])
        store(a_v.at[p], a_o.at[p])
        for copy in q_copies:
            copy.wait_recv()
        attention(p)
        store(qkv_v.at[p], qkv_o.at[p])
        store(o32_v.at[p], o32_o.at[p])
        store(lse_v.at[p], lse_o.at[p])
        if p == 0:
            loads[2].wait()
            e_copy.wait_send()
            cot_copy.start()
        for pair in range(pairs):
            o_copy(p, pair).wait_recv()
        m_v[p] = x_v[p] + dot(o_v[p], wout_v[...])

        def norm_two(rows):
            xh, _ = norm_parts(m_v[p, rows, :])
            b_v[p, rows, :] = low(xh * gain2)

        by_rows(tokens, norm_two)
        store(o_v.at[p], o_o.at[p])
        store(m_v.at[p], m_o.at[p])
        store(b_v.at[p], b_o.at[p])
        if p == 0:
            loads[3].wait()
            loads[4].wait()
        h_v[...] = m_v[p]

        for t in range(hidden_units // width):
            cols = slice(t * width, (t + 1) * width)
            u = dot(b_v[p], wup_v[:, cols])
            squared = u * u
            tan = jnp.tanh(u * (GELU_A + (GELU_A * GELU_B) * squared))
            upper = 0.5 + 0.5 * tan
            g_v[p, :, cols] = low(u * upper)
            slope = (0.5 * u) * (1.0 - tan * tan) * (GELU_A + (3.0 * GELU_A * GELU_B) * squared)
            gp_v[p, :, cols] = low(upper + slope)
            store(g_v.at[p, :, cols], g_o.at[p, :, cols])
            store(gp_v.at[p, :, cols], gp_o.at[p, :, cols])
            if t > 0:
                before = slice((t - 1) * width, t * width)
                h_v[...] += dot(g_v[p, :, before], wdown_v[before, :])
        h_v[...] += dot(g_v[p, :, hidden_units - width :], wdown_v[hidden_units - width :, :])
        hid_v[p] = low(h_v[...])
        store(hid_v.at[p], hid_o.at[p])

    cot_copy.wait()
    for p in range(2):
        for c in range(3):
            pltpu.make_async_remote_copy(
                own_qkv.at[p, c, :, pl.ds(aligned(half * (1 - r)), half)],
                qkv_v.at[p, c, pl.ds(aligned(tokens * r, 16), tokens), :],
                q_send.at[p, c], q_recv.at[p, c], device_id=core, device_id_type=MESH).wait_send()
        for pair in range(pairs):
            o_copy(p, pair).wait_send()
    for copy in stores:
        copy.wait()


class Route:
    def __init__(self, bits, late):
        self.bits = bits
        self.late = late

    def weights(self, r):
        n = self.bits
        if self.late:
            low_unit, rest = 1, [2 ** (n + 1 - b) for b in range(2, n)]
        else:
            low_unit, rest = 2 ** (n - 2), [2 ** (n - 1 - b) for b in range(2, n)]
        return [low_unit * (2 - r), low_unit * (1 + r)] + rest

    def slot(self, s_bits, my_bits, weights):
        total = 0
        for a, b, w in zip(s_bits, my_bits, weights):
            total = total + w * (1 - b if a else b)
        return total

    def partner(self, k, mates, r):
        n = self.bits
        at = k + 2 if self.late else k
        if self.late and k >= n - 2:
            at = k - (n - 2)
        if at > 1:
            return mates[at]
        return mates[at] + r * (mates[1 - at] - mates[at])


START = {
    "wd2": ("d0.0",), "wd3": ("d1.0",), "units": ("d2.0", "d3.0"), "wu2": ("u0.0",), "wu3": ("u1.0",), "db": ("u2.0",),
    "ln2": ("u3.0",), "dswait": ("o.0",), "wq2": ("q0.0",), "da": ("q1.0", "q2.0"),
}
PLAN = {
    "wd2": ("d0.0",),
    "wd3": ("d1.0",),
    "units": ("d2.0", "d3.0"),
    "wu2": ("u0.0",),
    "wu3": ("d0.1",),
    "db": ("u2.0", "u1.0"),
    "do": ("d1.1",),
    "at0": ("d3.1", "d2.1"),
    "at1": ("u0.1", "d1.2", "u3.0"),
    "at2": ("d0.2", "u2.1", "d3.2", "d2.2", "u1.1", "dz.0"),
    "wo": ("u3.1",),
    "dswait": ("o.0",),
    "wq1": ("u0.2", "q0.0", "u1.2"),
    "wq2": ("u2.2", "q1.0"),
    "da": ("u3.2", "q2.0", "dz.1"),
    "ln1": ("u1.3", "u0.3", "o.1", "g.1"),
    "end": ("u2.3", "u0.4", "u3.3", "u1.4", "g.2", "q0.1", "u3.4", "q1.1", "dz.2", "g.3", "o.2", "q2.1",
        "q0.2", "q1.2", "u2.4", "g.4", "o.3", "q2.2", "q0.3", "q1.3", "g.5", "q2.3", "q1.4", "o.4",
        "q0.4", "q2.4"),
}


def later_plan(parts, phases_of):
    low_parts = [n for n in parts if n[0] == "d" and n != "dz"]
    rest = [n for n in parts if n[0] != "d"]
    steps = [f"{n}.{k}" for k in range(1, phases_of("d0") + 1) for n in low_parts] + ["dz.0", "dz.1", "dz.2"]
    for k in range(1, phases_of("o") + 1):
        steps += [f"g.{k}"] + [f"{n}.{k}" for n in rest]
    return START | {"end": steps + [f"g.{phases_of('o') + 1}"]}


def backward_kernel(
    bits,
    hid_i, cot, cotx, seg, gain1_ref, gain2_ref, wqkv, wout, wup, wdown, x_i, a_i, qkv_i, o32_i, o_i, m_i, b_i, g_i, gp_i, lse_i,
    hidden, sgrad, gout, gqkv, gwout, gup, gdown,
    wqkv_v, wout_v, wup_v, wdown_v, m_v, o32_v, qkv_v, lse_v, b_v, g_v,
    df_v, du_v, dc_v, ds_v, do_own, do_v, dd_v, dm_v, dn_v, bias, dkv0, ds_tmp,
    sg_send_v, sg_recv_v,
    tile, send_v, own_v, stage, phd, phz, pho, gs, gr,
    in_sem, hid_sem, sg_sem, sg_local, do_sem, ds_send, ds_recv, c_send, c_recv, rs_send, rs_recv, f_send, f_recv, gain_sem,
):
    r, s, m = place()
    tokens, width = df_v.shape[1:]
    half = width // 2
    hidden_units = wup_v.shape[1]
    tiles = hidden_units // width
    pairs = half // PAIR
    sections = 2 ** bits
    rb = width // sections
    core = (s, 1 - r)
    relay = (s + 1 - 2 * m, r)
    n_in = 0

    def load(src, dst, at):
        copy = pltpu.make_async_copy(src, dst, in_sem.at[at])
        copy.start()
        return copy

    my_bits = [lax.rem(lax.div(s, 2 ** b), 2) for b in range(bits)]
    sections_near = [s + (1 - 2 * my_bits[b]) * 2 ** b for b in range(bits)]
    barrier = pltpu.get_barrier_semaphore()
    mates = [core]
    for b in range(bits):
        mates.append((sections_near[b], r))
    for mate in mates:
        pl.semaphore_signal(barrier, inc=1, device_id=mate, device_id_type=MESH)

    own_pass = load(cot.at[0, m], df_v.at[m], 0)
    other_pass = load(cotx, df_v.at[1 - m], 1)
    blocks = [pl.ds(t * width, width) for t in range(tiles)]
    ld_first = [(load(wdown.at[b, :], wdown_v.at[b, :], 21 + 2 * t), load(gp_i.at[1, :, b], du_v.at[1, :, b], 22 + 2 * t))
                for t, b in enumerate(blocks)]
    ld_up = load(wup, wup_v, 4)
    ld_m1 = load(m_i.at[1], m_v, 17)
    fill_bias(seg, m, bias, tokens)
    masks = head_masks()
    gain1 = gain1_ref[...].astype(F32).reshape(1, width)
    gain2 = gain2_ref[...].astype(F32).reshape(1, width)
    gs[0] = jnp.zeros(gs.shape[1:], F32)
    pl.semaphore_wait(barrier, len(mates))
    hid_own = load(hid_i.at[m], sg_send_v, 5)
    hid_copy = pltpu.make_async_remote_copy(
        hid_i.at[1 - m], hidden.at[0, m], hid_sem.at[0], hid_sem.at[1], device_id=relay, device_id_type=MESH)
    hid_copy.start()

    near = Route(bits, False)
    far = Route(bits, True)
    inner = Route(bits - 2, False)
    weights_of = {(route, who): route.weights(r if who else 1 - r) for route in (near, far, inner) for who in (0, 1)}
    others = [f"u{t}" for t in range(tiles)] + ["o", "q0", "q1", "q2"]
    route_of = {name: far if name in ("u0", "u2",) else near for name in others}
    parts = [f"d{t}" for t in range(tiles)] + ["dz"] + others
    slot_of = {f"d{t}": t for t in range(tiles)} | {f"u{t}": t for t in range(tiles)} | {"o": 0, "q0": 1, "q1": 2, "q2": 3}

    def tile_place(t):
        low_bit, high_bit = my_bits[bits - 2], my_bits[bits - 1]
        return 2 * (1 - low_bit if t & 1 else low_bit) + (1 - high_bit if t >> 1 else high_bit)

    def chunk_of(name):
        return tile_place(int(name[1])) if name[0] == "d" else tiles + others.index(name)

    def phases_of(name):
        return 2 if name == "dz" else bits - 2 if name[0] == "d" else bits

    def place_of(name, b, who):
        if name[0] == "d":
            bits_of = [((b // tiles) >> k) & 1 for k in range(bits - 2)]
            return inner.slot(bits_of, my_bits, weights_of[inner, who]) * tiles + b % tiles
        route = route_of[name]
        return route.slot([(b >> k) & 1 for k in range(bits)], my_bits, weights_of[route, who])

    def put_tile(name, lhs, rhs):
        part = width // 2
        slot = slot_of[name]
        for piece in range(2):
            tile[...] = dot_tn(lhs(piece * part, part), rhs)
            for bb in range(sections // 2):
                b = piece * (sections // 2) + bb
                theirs, mine = place_of(name, b, 0), place_of(name, b, 1)
                rows = slice(bb * rb, (bb + 1) * rb)
                send_v[slot, theirs] = low(tile[rows, pl.ds(aligned(half * (1 - r)), half)])
                own_v[slot, mine] = low(tile[rows, pl.ds(aligned(half * r), half)])
        core_copy(name).start()

    def core_copy(name):
        at = parts.index(name)
        return pltpu.make_async_remote_copy(
            send_v.at[slot_of[name]], stage.at[chunk_of(name)], c_send.at[at], c_recv.at[at],
            device_id=core, device_id_type=MESH)

    def add_blocks(c, other, n):
        def step(j, carry):
            stage[c, j] = low(stage[c, j].astype(F32) + other[j].astype(F32))
            return carry

        lax.fori_loop(0, n, step, 0, unroll=min(4, n))

    def rs_copy(name, k):
        at = parts.index(name)
        size = sections >> (k + 1)
        if name == "dz":
            mate = sections_near[bits - 2 + k]
            src, dst = (stage.at[2:4, 0:tiles], phz[0]) if k == 0 else (stage.at[1, 0:tiles], phz[1])
        elif name[0] == "d":
            mate = inner.partner(k, sections_near, r)
            src, dst = stage.at[chunk_of(name), pl.ds(size, size)], phd[k].at[int(name[1])]
        else:
            mate = route_of[name].partner(k, sections_near, r)
            src, dst = stage.at[chunk_of(name), pl.ds(size, size)], pho[k].at[others.index(name)]
        return pltpu.make_async_remote_copy(
            src, dst, rs_send.at[at, k], rs_recv.at[at, k], device_id=(mate, r), device_id_type=MESH)

    def rs_step(name, k):
        if k > 0:
            rs_copy(name, k - 1).wait_recv()
        if name == "dz":
            if k == 1:
                for c in range(2):
                    add_blocks(c, phz[0].at[c], tiles)
            if k == 2:
                for q in range(tiles):
                    total = stage[0, q].astype(F32) + phz[1][q].astype(F32)
                    gdown[q * rb : (q + 1) * rb, pl.ds(aligned(half * r), half)] = total
        elif name[0] == "d":
            if k > 0:
                add_blocks(chunk_of(name), phd[k - 1].at[int(name[1])], sections >> k)
        elif k > 0:
            at = others.index(name)
            if k < bits:
                add_blocks(tiles + at, pho[k - 1].at[at], sections >> k)
            else:
                view = final_view(name)
                view[...] = stage[tiles + at, 0].astype(F32) + pho[k - 1][at, 0].astype(F32)
        if k < phases_of(name):
            rs_copy(name, k).start()
        elif name == "dz" or name[0] != "d":
            final_copy(name).start()

    def final_view(name):
        if name == "dz":
            return gdown.at[:, pl.ds(aligned(half * r), half)]
        out = {"u": gup, "o": gwout, "q": gqkv}[name[0]]
        c = int(name[1]) if len(name) > 1 else 0
        return out.at[:, pl.ds(aligned(c * width + half * r), half)]

    def final_copy(name):
        at = parts.index(name)
        return pltpu.make_async_remote_copy(
            final_view(name), final_view(name), f_send.at[at], f_recv.at[at], device_id=core, device_id_type=MESH)

    plan = PLAN if bits == 4 else later_plan(parts, phases_of)

    def at(point):
        for item in plan.get(point, ()):
            name, k = item.split(".")
            if name == "g":
                gain_step(int(k))
                continue
            if k == "0" and name != "dz":
                core_copy(name).wait()
                add_blocks(chunk_of(name), own_v.at[slot_of[name]], sections)
            rs_step(name, int(k))

    def gain_copy(k):
        mate = mates[k]
        return pltpu.make_async_remote_copy(
            gs.at[k], gr.at[k], gain_sem.at[0, k], gain_sem.at[1, k], device_id=mate, device_id_type=MESH)

    def gain_step(k):
        if k > 0:
            gain_copy(k - 1).wait_recv()
            gs[k] = gs[k - 1] + gr[k - 1]
        if k <= bits:
            gain_copy(k).start()
        else:
            gout[...] = gs[k]

    def do_copy(p):
        return pltpu.make_async_remote_copy(
            do_own.at[:, pl.ds(aligned(half * (1 - r)), half)], do_v.at[p, pl.ds(aligned(tokens * r, 16), tokens), :],
            do_sem.at[0, p], do_sem.at[1, p], device_id=core, device_id_type=MESH)

    def ds_copy(p, pair, sending):
        at = r if sending else 1 - r
        cols = pl.ds(aligned(half * at + PAIR * pair), PAIR)
        return pltpu.make_async_remote_copy(
            ds_tmp.at[pair, :, 1 - r], ds_v.at[:, pl.ds(p * tokens, tokens), cols], ds_send.at[p, pair],
            ds_recv.at[p, pair], device_id=core, device_id_type=MESH)

    def attention_pair(p, pair):
        off = aligned(pair * PAIR)
        cols = pl.ds(off, PAIR)
        room = width // PAIR

        def acc(src, j, kv):
            a = (2 * src + j) * 2 + kv
            if a < room:
                return dn_v.at[:, a * PAIR : (a + 1) * PAIR]
            return tile.at[0:tokens, (a - room) * PAIR : (a - room + 1) * PAIR]

        for src in range(p + 1):
            for j in range(2):
                for kv in range(2):
                    acc(src, j, kv)[...] = jnp.zeros((tokens, PAIR), F32)
        for i in range(2):
            rows = slice(i * tokens, (i + 1) * tokens)
            q = qkv_v[p, 0, rows, cols]
            g = do_v[p, rows, cols]
            dq = None
            for h in range(2):
                q_h = q * masks[h]
                g_h = g * masks[h]
                lse = lse_v[p, 2 * pair + h, :, rows]
                dd = dd_v[2 * pair + h, :, rows]
                for src in range(p + 1):
                    for j in range(i + 1):
                        at = slice(j * tokens, (j + 1) * tokens)
                        key = qkv_v[src, 1, at, cols]
                        value = qkv_v[src, 2, at, cols]
                        prob = jnp.exp(dot_nt(key, q_h) + bias[i + j] - lse)
                        d_prob = dot_nt(value, g_h)
                        d_score = low(prob * (d_prob - dd))
                        acc(src, j, 0)[...] += dot(d_score, q_h)
                        acc(src, j, 1)[...] += dot(low(prob), g_h)
                        term = dot_tn(d_score, key * masks[h])
                        dq = term if dq is None else dq + term
            ds_tmp[pair, 0, i] = low(dq * (HEAD ** -0.5))
        for j in range(2):
            at = slice(j * tokens, (j + 1) * tokens)
            for kv in range(2):
                if p == 1:
                    dkv0[kv, at, cols] = acc(0, j, kv)[...]
                    ds_tmp[pair, 1 + kv, j] = low(acc(1, j, kv)[...])
                else:
                    ds_tmp[pair, 1 + kv, j] = low(acc(0, j, kv)[...] + dkv0[kv, at, cols])
        mine = pl.ds(aligned(half * r + off), PAIR)
        for c in range(3):
            ds_v[c, pl.ds(p * tokens, tokens), mine] = ds_tmp[pair, c, r]
        ds_copy(p, pair, True).start()

    def sg_own_copy():
        return pltpu.make_async_copy(dm_v, sgrad.at[0, m], sg_local.at[0])

    head_row = lax.broadcasted_iota(jnp.int32, (16, half), 0)
    head_of = lax.broadcasted_iota(jnp.int32, (16, half), 1)
    picks = low(jnp.where((head_of >= head_row * HEAD) & (head_of < (head_row + 1) * HEAD), 1.0, 0.0))

    own_pass.wait()
    other_pass.wait()

    for p in (1, 0):
        if p == 0:
            def join(rows):
                total = df_v[0, rows, :].astype(F32) + low(dm_v[rows, :]).astype(F32)
                dn_v[rows, :] = total
                df_v[0, rows, :] = low(total)

            by_rows(tokens, join)
            ld_gp0.wait()
            ld_g.wait()
            at("join")
            for t in range(tiles):
                put_tile(f"d{t}", lambda at, n: g_v[:, :, t * width + at : t * width + at + n].reshape(2 * tokens, n),
                         df_v[...].reshape(2 * tokens, width))
                at(f"wd{t}")
        for t, cols in enumerate(blocks):
            if p == 1:
                ld_first[t][0].wait()
                ld_first[t][1].wait()
            dg = dot_nt(df_v[p], wdown_v[cols, :])
            du_v[p, :, cols] = low(dg * du_v[p, :, cols].astype(F32))
        if p == 1:
            ld_up.wait()
            ld_m1.wait()
            ld_out = load(wout, wout_v, 6)
            ld_qkv = load(qkv_i, qkv_v, 7)
            ld_o32 = load(o32_i.at[1], o32_v, 8)
            ld_lse = load(lse_i, lse_v, 9)
        else:
            ld_o = load(o_i, df_v, 15)
            ld_m0.wait()

            @pl.when(m == 1)
            def _():
                sg_own_copy().wait()

            at("units")
            ld_b.wait()
            for t in range(tiles):
                put_tile(f"u{t}", lambda at, n: b_v[:, :, at : at + n].reshape(2 * tokens, n),
                         du_v[:, :, t * width : (t + 1) * width].reshape(2 * tokens, width))
                at(f"wu{t}")
            ld_a = load(a_i, b_v, 16)
        dm_v[...] = dot_nt(du_v[p], wup_v[...])
        if p == 0:
            at("db")

        def norm_two_back(rows):
            xh, scale = norm_parts(m_v[rows, :])
            dy = dm_v[rows, :]
            gs[0, 1:2, :] += jnp.sum(dy * xh, axis=0, keepdims=True)
            dxh = dy * gain2
            dv = scale * (dxh - mean_of(dxh) - xh * mean_of(dxh * xh))
            grad = df_v[1, rows, :].astype(F32) if p == 1 else dn_v[rows, :]
            total = grad + dv
            dm_v[rows, :] = total
            dc_v[p, rows, :] = low(total)

        by_rows(tokens, norm_two_back)
        ld_x = load(x_i.at[p], m_v, 11 + p)
        if p == 1:
            ld_out.wait()
            ld_wqkv = load(wqkv, wqkv_v, 10)
        else:
            at("ln2")
            do_copy(1).wait_send()
        do_own[...] = low(dot_nt(dc_v[p], wout_v[...]))
        do_copy(p).start()
        do_v[p, pl.ds(aligned(tokens * r, 16), tokens), :] = do_own[:, pl.ds(aligned(half * r), half)]
        if p == 1:
            ld_qkv.wait()
            ld_lse.wait()
            ld_o32.wait()
            ld_gp0 = load(gp_i.at[0], du_v.at[0], 18)
            hid_own.wait()
            hid_out = pltpu.make_async_copy(sg_send_v, hidden.at[0, m], in_sem.at[5])
            hid_out.start()
            ld_g = load(g_i, g_v, 13)
            ld_b = load(b_i, b_v, 14)
        else:
            at("do")
            ld_o320.wait()
        do_copy(p).wait_recv()
        for i in range(2):
            rows = slice(i * tokens, (i + 1) * tokens)
            prod = do_v[p, rows, :].astype(F32) * o32_v[rows, :]
            upper = low(prod)
            rest = low(prod - upper.astype(F32))
            sums = dot_nt(picks, upper) + dot_nt(picks, rest)
            for h in range(2 * pairs):
                dd_v[h, :, rows] = sums[h : h + 1, :]
        if p == 1:
            ld_o320 = load(o32_i.at[0], o32_v, 20)

            def pair_step(pair, carry):
                attention_pair(1, pair)
                return carry

            lax.fori_loop(0, pairs, pair_step, 0)
        else:
            at("dowait")
            for pair in range(pairs):
                ds_copy(1, pair, True).wait_send()
            for pair in range(pairs):
                attention_pair(0, pair)
                at(f"at{pair}")
            ld_o.wait()
            put_tile("o", lambda at, n: df_v[:, :, at : at + n].reshape(2 * tokens, n), dc_v[...].reshape(2 * tokens, width))
            at("wo")
            ld_a.wait()
        for pair in range(pairs):
            ds_copy(p, pair, False).wait_recv()
        if p == 1:
            ld_wqkv.wait()
        else:
            at("dswait")
            for c in range(3):
                put_tile(f"q{c}", lambda at, n: b_v[:, :, at : at + n].reshape(2 * tokens, n), ds_v[c])
                at(f"wq{c}")
        ld_x.wait()
        for c in range(3):
            term = dot_nt(ds_v[c, p * tokens : (p + 1) * tokens, :], wqkv_v[:, c * width : (c + 1) * width])
            dn_v[...] = term if c == 0 else dn_v[...] + term
        if p == 0:
            at("da")

        def norm_one_back(rows):
            xh, scale = norm_parts(m_v[rows, :])
            dy = dn_v[rows, :]
            gs[0, 0:1, :] += jnp.sum(dy * xh, axis=0, keepdims=True)
            dxh = dy * gain1
            dv = scale * (dxh - mean_of(dxh) - xh * mean_of(dxh * xh))
            dm_v[rows, :] = dm_v[rows, :] + dv

        by_rows(tokens, norm_one_back)

        if p == 1:
            hid_out.wait()

        @pl.when(m == p)
        def _():
            sg_own_copy().start()

        @pl.when(m != p)
        def _():
            sg_send_v[...] = low(dm_v[...])
            pltpu.make_async_remote_copy(
                sg_send_v, sg_recv_v, sg_sem.at[0], sg_sem.at[1], device_id=relay, device_id_type=MESH).start()

        if p == 1:
            ld_m0 = load(m_i.at[0], m_v, 19)

    gain_step(0)
    at("ln1")
    at("end")
    sg_copy = pltpu.make_async_remote_copy(
        sg_send_v, sg_recv_v, sg_sem.at[0], sg_sem.at[1], device_id=relay, device_id_type=MESH)
    sg_copy.wait_recv()
    dn_v[...] = sg_recv_v[...].astype(F32)
    sg_last = pltpu.make_async_copy(dn_v, sgrad.at[0, 1 - m], sg_local.at[1])
    sg_last.start()

    for name in parts:
        if name == "dz" or name[0] != "d":
            final_copy(name).wait()
        for k in range(phases_of(name)):
            rs_copy(name, k).wait_send()
    hid_copy.wait()
    for k in range(bits + 1):
        gain_copy(k).wait_send()
    do_copy(0).wait_send()
    for pair in range(pairs):
        ds_copy(0, pair, True).wait_send()
    sg_copy.wait_send()

    @pl.when(m == 0)
    def _():
        sg_own_copy().wait()

    sg_last.wait()


def shape(dims, dtype):
    return jax.ShapeDtypeStruct(dims, dtype)


def forward_call(stream, cot, seg, gains, weights):
    wqkv, wout, wup, wdown = weights
    _, _, tokens, width = stream.shape
    units = wup.shape[1]
    half = width // 2
    length = 2 * tokens
    pairs = half // PAIR
    saved = [
        shape((2, tokens, width), F32),
        shape((2, tokens, width), BF16),
        shape((2, 3, length, half), BF16),
        shape((2, length, half), F32),
        shape((2, tokens, width), BF16),
        shape((2, tokens, width), F32),
        shape((2, tokens, width), BF16),
        shape((2, tokens, units), BF16),
        shape((2, tokens, units), BF16),
        shape((2, 2 * pairs, 1, length), F32),
    ]
    anyspace = pl.BlockSpec(memory_space=pl.ANY)
    vmem = pl.BlockSpec(memory_space=pltpu.VMEM)
    V = pltpu.VMEM
    sem = pltpu.SemaphoreType.DMA
    return pl.pallas_call(
        forward_kernel,
        out_shape=[shape((2, tokens, width), BF16), shape((tokens, width), BF16)] + saved,
        in_specs=[anyspace, anyspace, vmem, vmem, vmem] + [anyspace] * 4,
        out_specs=[anyspace] * 12,
        scratch_shapes=[
            V(wqkv.shape, BF16), V(wout.shape, BF16), V(wup.shape, BF16), V(wdown.shape, BF16),
            V((tokens, width), BF16), V((tokens, width), BF16), V((2, tokens, width), F32),
            V((2, tokens, width), BF16), V((2, 3, tokens, width), BF16), V((2, 3, length, half), BF16),
            V((2, length, half), F32), V((2, pairs, 2, tokens, PAIR), BF16), V((2, tokens, width), BF16),
            V((2, tokens, width), F32), V((2, tokens, width), BF16), V((2, tokens, units), BF16),
            V((2, tokens, units), BF16), V((tokens, width), F32), V((2, tokens, width), BF16),
            V((2, 2 * pairs, 1, length), F32), V((3, tokens, tokens), F32),
            sem((5,)), sem((2 * (9 + 2 * (units // width)),)), sem((2,)), sem((2,)),
            sem((2, 3)), sem((2, 3)), sem((2, pairs)), sem((2, pairs)),
        ],
        compiler_params=pltpu.CompilerParams(collective_id=0, has_side_effects=True, vmem_limit_bytes=VMEM_LIMIT),
        name="forward",
    )(stream, cot, seg, *gains, wqkv, wout, wup, wdown)


def backward_call(hid, cot, cotx, seg, gains, weights, saved, sections):
    wqkv, wout, wup, wdown = weights
    _, _, tokens, width = cot.shape
    units = wup.shape[1]
    half = width // 2
    length = 2 * tokens
    pairs = half // PAIR
    tiles = units // width
    chunks = 2 * tiles + 4
    bits = sections.bit_length() - 1
    assert 2 ** bits == sections and bits >= 4 and tiles == 4
    rb = width // sections
    anyspace = pl.BlockSpec(memory_space=pl.ANY)
    vmem = pl.BlockSpec(memory_space=pltpu.VMEM)
    V = pltpu.VMEM
    sem = pltpu.SemaphoreType.DMA

    def body(*refs):
        fixed = len(scratch) + 20 + 7
        phd, refs_z = refs[fixed : fixed + bits - 2], refs[fixed + bits - 2 :]
        phz, pho, rest = refs_z[:2], refs_z[2 : 2 + bits], refs_z[2 + bits :]
        backward_kernel(bits, *refs[:fixed], phd, phz, pho, *rest)

    scratch = [
        V(wqkv.shape, BF16), V(wout.shape, BF16), V(wup.shape, BF16), V(wdown.shape, BF16),
        V((tokens, width), F32), V((length, half), F32),
        V((2, 3, length, half), BF16), V((2, 2 * pairs, 1, length), F32),
        V((2, tokens, width), BF16), V((2, tokens, units), BF16),
        V((2, tokens, width), BF16), V((2, tokens, units), BF16), V((2, tokens, width), BF16),
        V((3, 2 * tokens, width), BF16), V((tokens, width), BF16), V((2, length, half), BF16),
        V((2 * pairs, 1, length), F32), V((tokens, width), F32), V((tokens, width), F32),
        V((3, tokens, tokens), F32), V((2, length, half), F32),
        V((pairs, 3, 2, tokens, PAIR), BF16),
        V((tokens, width), BF16), V((tokens, width), BF16),
        V((width // 2, width), F32), V((tiles, sections, rb, half), BF16), V((tiles, sections, rb, half), BF16),
        V((chunks, sections, rb, half), BF16),
    ]
    ph = [V((tiles, sections >> (k + 1), rb, half), BF16) for k in range(bits - 2)]
    ph += [V((2, tiles, rb, half), BF16), V((tiles, rb, half), BF16)]
    ph += [V((chunks - tiles, sections >> (k + 1), rb, half), BF16) for k in range(bits)]
    rest = [
        V((bits + 2, 8, width), F32), V((bits + 1, 8, width), F32),
        sem((21 + 2 * tiles,)), sem((2,)), sem((2,)), sem((2,)), sem((2, 2)), sem((2, pairs)), sem((2, pairs)),
        sem((chunks + 1,)), sem((chunks + 1,)), sem((chunks + 1, bits)), sem((chunks + 1, bits)),
        sem((chunks + 1,)), sem((chunks + 1,)), sem((2, bits + 1)),
    ]
    return pl.pallas_call(
        body,
        out_shape=[
            shape(cot.shape, BF16), shape(cot.shape, F32), shape((8, width), F32), shape((rb, 3 * width), F32), shape((rb, width), F32),
            shape((rb, units), F32), shape((tiles * rb, width), F32),
        ],
        in_specs=[anyspace, anyspace, anyspace, vmem, vmem, vmem] + [anyspace] * 14,
        out_specs=[anyspace] * 2 + [vmem] * 5,
        scratch_shapes=scratch + ph + rest,
        compiler_params=pltpu.CompilerParams(collective_id=1, has_side_effects=True, vmem_limit_bytes=VMEM_LIMIT),
        name="backward",
    )(hid, cot, cotx, seg, *gains, wqkv, wout, wup, wdown, *saved)


def finish_kernel(sections, gout, *refs):
    n = (len(refs) - 3) // 3
    sources, targets, gain1, gain2 = refs[:n], refs[n : 2 * n], refs[2 * n], refs[2 * n + 1]
    held, sem = refs[2 * n + 2 : -1], refs[-1]
    ins = [pltpu.make_async_copy(a, b, sem.at[0, i]) for i, (a, b) in enumerate(zip(sources, held))]
    outs = [pltpu.make_async_copy(a, b, sem.at[1, i]) for i, (a, b) in enumerate(zip(held, targets))]
    for copy in ins:
        copy.start()
    width = gout.shape[1]
    rb = width // sections
    s = lax.axis_index("section")
    turned = pltpu.roll(gout[...], lax.rem(width - s * rb, width), 1)
    gain1[...] = turned[0, :rb]
    gain2[...] = turned[1, :rb]
    for arrived, copy in zip(ins, outs):
        arrived.wait()
        copy.start()
    for copy in outs:
        copy.wait()


def finish_call(gout, arrays, sections):
    anyspace = pl.BlockSpec(memory_space=pl.ANY)
    vmem = pl.BlockSpec(memory_space=pltpu.VMEM)
    gain = shape((gout.shape[1] // sections,), F32)
    return pl.pallas_call(
        functools.partial(finish_kernel, sections),
        out_shape=[shape(a.shape, a.dtype) for a in arrays] + [gain, gain],
        in_specs=[vmem] + [anyspace] * len(arrays),
        out_specs=[anyspace] * len(arrays) + [vmem, vmem],
        scratch_shapes=[pltpu.VMEM(a.shape, a.dtype) for a in arrays] + [pltpu.SemaphoreType.DMA((2, len(arrays)))],
        compiler_params=pltpu.CompilerParams(vmem_limit_bytes=VMEM_LIMIT),
        name="finish",
    )(gout, *arrays)


def per_device(stream, segment_ids, ln1_gain, w_qkv, w_out, ln2_gain, w_up, w_down, cotangent):
    sections = lax.axis_size("section")
    gains = (ln1_gain, ln2_gain)
    weights = (w_qkv, w_out, w_up, w_down)
    hid, cotx, *saved = forward_call(stream, cotangent, segment_ids, gains, weights)
    hidden, sgrad, gout, gqkv, gwout, gup, gdown = backward_call(hid, cotangent, cotx, segment_ids, gains, weights, saved, sections)
    hidden, sgrad, gqkv, gwout, gup, gdown, gain1, gain2 = finish_call(
        gout, (hidden, sgrad, gqkv, gwout, gup, gdown), sections)
    return (hidden, sgrad, gain1, gqkv, gwout, gain2, gup, gdown)


def solution(mesh):
    rows = P("section", None, "rows", None)
    assert mesh.shape["rows"] == 2
    return jax.shard_map(
        per_device,
        mesh=mesh,
        in_specs=(rows, P("section", None, None), P(), P(), P(), P(), P(), P(), rows),
        out_specs=(rows, rows, P("section"), P("section", None), P("section", None), P("section"),
                   P("section", None), P("section", None)),
        check_vma=False,
    )
```

```python
import functools

import jax
import jax.numpy as jnp
from jax import lax
from jax.experimental import pallas as pl
from jax.experimental.pallas import tpu as pltpu
from jax.sharding import PartitionSpec as P

HEAD = 64
PAIR = 128
EPS = 1e-05
MASKED = -1e30
F32 = jnp.float32
BF16 = jnp.bfloat16
MESH = pl.DeviceIdType.MESH
GELU_A = 0.7978845608
GELU_B = 0.044715
CHUNK = 64
VMEM_LIMIT = 65300 * 1024


def dot(a, b):
    return jnp.dot(a, b, preferred_element_type=F32)


def dot_nt(a, b):
    return lax.dot_general(a, b, (((1,), (1,)), ((), ())), preferred_element_type=F32)


def dot_tn(a, b):
    return lax.dot_general(a, b, (((0,), (0,)), ((), ())), preferred_element_type=F32)


def low(v):
    return v.astype(BF16)


def mean_of(v):
    return jnp.sum(v, axis=-1, keepdims=True) * (1.0 / v.shape[-1])


def norm_parts(v):
    centered = v - mean_of(v)
    scale = lax.rsqrt(mean_of(centered * centered) + EPS)
    return centered * scale, scale


def by_rows(rows, body):
    def step(i, carry):
        body(pl.ds(pl.multiple_of(i * CHUNK, CHUNK), CHUNK))
        return carry

    lax.fori_loop(0, rows // CHUNK, step, 0, unroll=True)


def place():
    r = lax.axis_index("rows")
    s = lax.axis_index("section")
    m = lax.rem(s, 2)
    return r, s, m


def aligned(value, unit=128):
    return value if isinstance(value, int) else pl.multiple_of(value, unit)


def head_masks():
    lane = lax.broadcasted_iota(jnp.int32, (1, PAIR), 1)
    first = jnp.where(lane < HEAD, 1.0, 0.0)
    return low(first), low(1.0 - first)


def fill_bias(seg_ref, m, bias, tokens):
    length = 2 * tokens
    row = seg_ref[0, pl.ds(m, 1), :].astype(F32)
    col = jnp.broadcast_to(row, (PAIR, length)).T
    key_at = lax.broadcasted_iota(jnp.int32, (tokens, tokens), 0)
    query_at = lax.broadcasted_iota(jnp.int32, (tokens, tokens), 1)
    for i, j in ((0, 0), (1, 0), (1, 1)):
        seen = col[j * tokens : (j + 1) * tokens, :1] == row[:, i * tokens : (i + 1) * tokens]
        if i == j:
            seen = seen & (key_at <= query_at)
        bias[i + j] = jnp.where(seen, 0.0, MASKED).astype(bias.dtype)


def forward_kernel(
    stream, cot, seg, gain1_ref, gain2_ref, wqkv, wout, wup, wdown,
    hid_o, cotx, x_o, a_o, qkv_o, o32_o, o_o, m_o, b_o, g_o, gp_o, lse_o,
    wqkv_v, wout_v, wup_v, wdown_v, e_own, e_recv, x_v, a_v, own_qkv, qkv_v, o32_v, o_tmp, o_v,
    m_v, b_v, g_v, gp_v, h_v, hid_v, lse_v, bias,
    in_sem, out_sem, e_sem, cot_sem, q_send, q_recv, o_send, o_recv,
):
    r, s, m = place()
    tokens, width = e_own.shape
    half = width // 2
    hidden_units = wup_v.shape[1]
    pairs = half // PAIR
    core = (s, 1 - r)
    relay = (s + 1 - 2 * m, r)

    loads = [
        pltpu.make_async_copy(stream.at[0, m], e_own, in_sem.at[0]),
        pltpu.make_async_copy(wqkv, wqkv_v, in_sem.at[1]),
        pltpu.make_async_copy(wout, wout_v, in_sem.at[2]),
        pltpu.make_async_copy(wup, wup_v, in_sem.at[3]),
        pltpu.make_async_copy(wdown, wdown_v, in_sem.at[4]),
    ]
    barrier = pltpu.get_barrier_semaphore()
    pl.semaphore_signal(barrier, inc=1, device_id=core, device_id_type=MESH)
    pl.semaphore_signal(barrier, inc=1, device_id=relay, device_id_type=MESH)
    for load in loads:
        load.start()
    pl.semaphore_wait(barrier, 2)

    e_copy = pltpu.make_async_remote_copy(
        stream.at[0, 1 - m], e_recv, e_sem.at[0], e_sem.at[1], device_id=relay, device_id_type=MESH)
    e_copy.start()
    cot_copy = pltpu.make_async_remote_copy(
        cot.at[0, 1 - m], cotx, cot_sem.at[0], cot_sem.at[1], device_id=relay, device_id_type=MESH)

    fill_bias(seg, m, bias, tokens)
    masks = head_masks()
    stores = []

    def store(src, dst):
        copy = pltpu.make_async_copy(src, dst, out_sem.at[len(stores)])
        copy.start()
        stores.append(copy)

    def attention(p):
        lane = lax.broadcasted_iota(jnp.int32, (tokens, PAIR), 1)

        def pair_step(pair, carry):
            off = aligned(pair * PAIR)
            cols = pl.ds(off, PAIR)
            for i in range(2):
                rows = slice(i * tokens, (i + 1) * tokens)
                q = qkv_v[p, 0, rows, cols]
                mixed = []
                for h in range(2):
                    q_h = q * masks[h]
                    scores, values = [], []
                    for src in range(p + 1):
                        for j in range(i + 1):
                            at = slice(j * tokens, (j + 1) * tokens)
                            scores.append(dot_nt(qkv_v[src, 1, at, cols], q_h) + bias[i + j])
                            values.append((src, at))
                    top = jnp.max(functools.reduce(jnp.maximum, scores), axis=0, keepdims=True)
                    expo = [jnp.exp(z - top) for z in scores]
                    total = jnp.sum(functools.reduce(jnp.add, expo), axis=0, keepdims=True)
                    share = 1.0 / total
                    out = None
                    for e, (src, at) in zip(expo, values):
                        term = dot_tn(low(e * share), qkv_v[src, 2, at, cols])
                        out = term if out is None else out + term
                    mixed.append(out)
                    lse_v[p, 2 * pair + h, :, rows] = top + jnp.log(total)
                both = jnp.where(lane < HEAD, mixed[0], mixed[1])
                o32_v[p, rows, cols] = both
                o_tmp[p, pair, i] = low(both)
            mine = pl.ds(aligned(half * r + off), PAIR)
            o_v[p, :, mine] = o_tmp[p, pair, r]
            pltpu.make_async_remote_copy(
                o_tmp.at[p, pair, 1 - r], o_v.at[p, :, mine], o_send.at[p, pair], o_recv.at[p, pair],
                device_id=core, device_id_type=MESH).start()
            return carry

        for pair in range(pairs):
            pair_step(pair, 0)

    def o_copy(p, pair):
        cols = pl.ds(aligned(half * (1 - r) + PAIR * pair), PAIR)
        return pltpu.make_async_remote_copy(
            o_tmp.at[p, pair, r], o_v.at[p, :, cols], o_send.at[p, pair], o_recv.at[p, pair],
            device_id=core, device_id_type=MESH)

    gain1 = gain1_ref[...].astype(F32).reshape(1, width)
    gain2 = gain2_ref[...].astype(F32).reshape(1, width)

    for p in range(2):
        if p == 0:
            loads[0].wait()

            @pl.when(m == 0)
            def _():
                x_v[0] = e_own[...].astype(F32)

            @pl.when(m == 1)
            def _():
                e_copy.wait_recv()
                x_v[0] = e_recv[...].astype(F32)
        else:
            @pl.when(m == 0)
            def _():
                e_copy.wait_recv()
                x_v[1] = hid_v[0].astype(F32) + e_recv[...].astype(F32)

            @pl.when(m == 1)
            def _():
                x_v[1] = hid_v[0].astype(F32) + e_own[...].astype(F32)

        def norm_one(rows):
            xh, _ = norm_parts(x_v[p, rows, :])
            a_v[p, rows, :] = low(xh * gain1)

        by_rows(tokens, norm_one)
        if p == 0:
            loads[1].wait()
        q_copies = []
        for c in range(3):
            tile = dot(a_v[p], wqkv_v[:, c * width : (c + 1) * width])
            tile = low(tile)
            if c == 0:
                tile = tile * low(jnp.full((1, 1), HEAD ** -0.5, F32))
            own_qkv[p, c] = tile
            their = pl.ds(aligned(half * (1 - r)), half)
            copy = pltpu.make_async_remote_copy(
                own_qkv.at[p, c, :, their], qkv_v.at[p, c, pl.ds(aligned(tokens * r, 16), tokens), :],
                q_send.at[p, c], q_recv.at[p, c], device_id=core, device_id_type=MESH)
            copy.start()
            q_copies.append(copy)
        for c in range(3):
            qkv_v[p, c, pl.ds(aligned(tokens * r, 16), tokens), :] = own_qkv[p, c, :, pl.ds(aligned(half * r), half)]
        store(x_v.at[p], x_o.at[p])
        store(a_v.at[p], a_o.at[p])
        for copy in q_copies:
            copy.wait_recv()
        attention(p)
        store(qkv_v.at[p], qkv_o.at[p])
        store(o32_v.at[p], o32_o.at[p])
        store(lse_v.at[p], lse_o.at[p])
        if p == 0:
            loads[2].wait()
            e_copy.wait_send()
            cot_copy.start()
        for pair in range(pairs):
            o_copy(p, pair).wait_recv()
        m_v[p] = x_v[p] + dot(o_v[p], wout_v[...])

        def norm_two(rows):
            xh, _ = norm_parts(m_v[p, rows, :])
            b_v[p, rows, :] = low(xh * gain2)

        by_rows(tokens, norm_two)
        store(o_v.at[p], o_o.at[p])
        store(m_v.at[p], m_o.at[p])
        store(b_v.at[p], b_o.at[p])
        if p == 0:
            loads[3].wait()
            loads[4].wait()
        h_v[...] = m_v[p]

        for t in range(hidden_units // width):
            cols = slice(t * width, (t + 1) * width)
            u = dot(b_v[p], wup_v[:, cols])
            squared = u * u
            tan = jnp.tanh(u * (GELU_A + (GELU_A * GELU_B) * squared))
            upper = 0.5 + 0.5 * tan
            g_v[p, :, cols] = low(u * upper)
            slope = (0.5 * u) * (1.0 - tan * tan) * (GELU_A + (3.0 * GELU_A * GELU_B) * squared)
            gp_v[p, :, cols] = low(upper + slope)
            store(g_v.at[p, :, cols], g_o.at[p, :, cols])
            store(gp_v.at[p, :, cols], gp_o.at[p, :, cols])
            if t > 0:
                before = slice((t - 1) * width, t * width)
                h_v[...] += dot(g_v[p, :, before], wdown_v[before, :])
        h_v[...] += dot(g_v[p, :, hidden_units - width :], wdown_v[hidden_units - width :, :])
        hid_v[p] = low(h_v[...])
        store(hid_v.at[p], hid_o.at[p])

    cot_copy.wait()
    for p in range(2):
        for c in range(3):
            pltpu.make_async_remote_copy(
                own_qkv.at[p, c, :, pl.ds(aligned(half * (1 - r)), half)],
                qkv_v.at[p, c, pl.ds(aligned(tokens * r, 16), tokens), :],
                q_send.at[p, c], q_recv.at[p, c], device_id=core, device_id_type=MESH).wait_send()
        for pair in range(pairs):
            o_copy(p, pair).wait_send()
    for copy in stores:
        copy.wait()


class Route:
    def __init__(self, bits, late):
        self.bits = bits
        self.late = late

    def weights(self, r):
        n = self.bits
        if self.late:
            low_unit, rest = 1, [2 ** (n + 1 - b) for b in range(2, n)]
        else:
            low_unit, rest = 2 ** (n - 2), [2 ** (n - 1 - b) for b in range(2, n)]
        return [low_unit * (2 - r), low_unit * (1 + r)] + rest

    def slot(self, s_bits, my_bits, weights):
        total = 0
        for a, b, w in zip(s_bits, my_bits, weights):
            total = total + w * (1 - b if a else b)
        return total

    def partner(self, k, mates, r):
        n = self.bits
        at = k + 2 if self.late else k
        if self.late and k >= n - 2:
            at = k - (n - 2)
        if at > 1:
            return mates[at]
        return mates[at] + r * (mates[1 - at] - mates[at])


START = {
    "wd2": ("d0.0",), "wd3": ("d1.0",), "units": ("d2.0", "d3.0"), "wu2": ("u0.0",), "wu3": ("u1.0",), "db": ("u2.0",),
    "ln2": ("u3.0",), "dswait": ("o.0",), "wq2": ("q0.0",), "da": ("q1.0", "q2.0"),
}
PLAN = {
    "wd3": ("d2.0", "d0.0", "d1.0", "d3.0"),
    "wu1": ("u0.0",),
    "do": ("u1.0", "u2.0", "d0.1", "d1.1"),
    "dowait": ("u3.0", "d2.1"),
    "at0": ("d3.1", "u0.1"),
    "at2": ("d1.2", "d0.2", "d2.2", "u1.1", "d3.2", "u3.1"),
    "wo": ("dz.0", "u2.1"),
    "dswait": ("o.0",),
    "wq1": ("u0.2", "q0.0"),
    "da": ("u2.2", "u1.2", "q1.0", "dz.1", "u3.2", "o.1", "q2.0", "u3.3", "u0.3"),
    "ln1": ("u1.3", "g.1"),
    "end": ("q0.1", "q1.1", "dz.2", "o.2", "g.2", "u2.3", "u1.4", "u3.4", "q2.1", "g.3", "q0.2", "u0.4",
        "o.3", "q1.2", "g.4", "q2.2", "q0.3", "q1.3", "q2.3", "g.5", "q0.4", "o.4", "u2.4", "q1.4",
        "q2.4"),
}


def later_plan(parts, phases_of):
    low_parts = [n for n in parts if n[0] == "d" and n != "dz"]
    rest = [n for n in parts if n[0] != "d"]
    steps = [f"{n}.{k}" for k in range(1, phases_of("d0") + 1) for n in low_parts] + ["dz.0", "dz.1", "dz.2"]
    for k in range(1, phases_of("o") + 1):
        steps += [f"g.{k}"] + [f"{n}.{k}" for n in rest]
    return START | {"end": steps + [f"g.{phases_of('o') + 1}"]}


def backward_kernel(
    bits,
    hid_i, cot, cotx, seg, gain1_ref, gain2_ref, wqkv, wout, wup, wdown, x_i, a_i, qkv_i, o32_i, o_i, m_i, b_i, g_i, gp_i, lse_i,
    hidden, sgrad, gout, gqkv, gwout, gup, gdown,
    wqkv_v, wout_v, wup_v, wdown_v, m_v, o32_v, qkv_v, lse_v, b_v, g_v,
    df_v, du_v, dc_v, ds_v, do_own, do_v, dd_v, dm_v, dn_v, bias, dkv0, ds_tmp,
    sg_send_v, sg_recv_v,
    tile, send_v, own_v, stage, phd, phz, pho, gs, gr,
    in_sem, hid_sem, sg_sem, sg_local, do_sem, ds_send, ds_recv, c_send, c_recv, rs_send, rs_recv, f_send, f_recv, gain_sem,
):
    r, s, m = place()
    tokens, width = df_v.shape[1:]
    half = width // 2
    hidden_units = wup_v.shape[1]
    tiles = hidden_units // width
    pairs = half // PAIR
    sections = 2 ** bits
    rb = width // sections
    core = (s, 1 - r)
    relay = (s + 1 - 2 * m, r)
    n_in = 0

    def load(src, dst, at):
        copy = pltpu.make_async_copy(src, dst, in_sem.at[at])
        copy.start()
        return copy

    my_bits = [lax.rem(lax.div(s, 2 ** b), 2) for b in range(bits)]
    sections_near = [s + (1 - 2 * my_bits[b]) * 2 ** b for b in range(bits)]
    barrier = pltpu.get_barrier_semaphore()
    mates = [core]
    for b in range(bits):
        mates.append((sections_near[b], r))
    for mate in mates:
        pl.semaphore_signal(barrier, inc=1, device_id=mate, device_id_type=MESH)

    own_pass = load(cot.at[0, m], df_v.at[m], 0)
    other_pass = load(cotx, df_v.at[1 - m], 1)
    blocks = [pl.ds(t * width, width) for t in range(tiles)]
    ld_first = [(load(wdown.at[b, :], wdown_v.at[b, :], 21 + 2 * t), load(gp_i.at[1, :, b], du_v.at[1, :, b], 22 + 2 * t))
                for t, b in enumerate(blocks)]
    ld_up = load(wup, wup_v, 4)
    ld_m1 = load(m_i.at[1], m_v, 17)
    fill_bias(seg, m, bias, tokens)
    masks = head_masks()
    gain1 = gain1_ref[...].astype(F32).reshape(1, width)
    gain2 = gain2_ref[...].astype(F32).reshape(1, width)
    gs[0] = jnp.zeros(gs.shape[1:], F32)
    pl.semaphore_wait(barrier, len(mates))
    hid_own = load(hid_i.at[m], sg_send_v, 5)
    hid_copy = pltpu.make_async_remote_copy(
        hid_i.at[1 - m], hidden.at[0, m], hid_sem.at[0], hid_sem.at[1], device_id=relay, device_id_type=MESH)
    hid_copy.start()

    near = Route(bits, False)
    far = Route(bits, True)
    inner = Route(bits - 2, False)
    weights_of = {(route, who): route.weights(r if who else 1 - r) for route in (near, far, inner) for who in (0, 1)}
    others = [f"u{t}" for t in range(tiles)] + ["o", "q0", "q1", "q2"]
    route_of = {name: far if name in ("u0", "u1",) else near for name in others}
    parts = [f"d{t}" for t in range(tiles)] + ["dz"] + others
    slot_of = {f"d{t}": t for t in range(tiles)} | {f"u{t}": t for t in range(tiles)} | {"o": 0, "q0": 1, "q1": 2, "q2": 3}

    def tile_place(t):
        low_bit, high_bit = my_bits[bits - 2], my_bits[bits - 1]
        return 2 * (1 - low_bit if t & 1 else low_bit) + (1 - high_bit if t >> 1 else high_bit)

    def chunk_of(name):
        return tile_place(int(name[1])) if name[0] == "d" else tiles + others.index(name)

    def phases_of(name):
        return 2 if name == "dz" else bits - 2 if name[0] == "d" else bits

    def place_of(name, b, who):
        if name[0] == "d":
            bits_of = [((b // tiles) >> k) & 1 for k in range(bits - 2)]
            return inner.slot(bits_of, my_bits, weights_of[inner, who]) * tiles + b % tiles
        route = route_of[name]
        return route.slot([(b >> k) & 1 for k in range(bits)], my_bits, weights_of[route, who])

    def put_tile(name, lhs, rhs):
        part = width // 2
        slot = slot_of[name]
        for piece in range(2):
            tile[...] = dot_tn(lhs(piece * part, part), rhs)
            for bb in range(sections // 2):
                b = piece * (sections // 2) + bb
                theirs, mine = place_of(name, b, 0), place_of(name, b, 1)
                rows = slice(bb * rb, (bb + 1) * rb)
                send_v[slot, theirs] = low(tile[rows, pl.ds(aligned(half * (1 - r)), half)])
                own_v[slot, mine] = low(tile[rows, pl.ds(aligned(half * r), half)])
        core_copy(name).start()

    def core_copy(name):
        at = parts.index(name)
        return pltpu.make_async_remote_copy(
            send_v.at[slot_of[name]], stage.at[chunk_of(name)], c_send.at[at], c_recv.at[at],
            device_id=core, device_id_type=MESH)

    def add_blocks(c, other, n):
        def step(j, carry):
            stage[c, j] = low(stage[c, j].astype(F32) + other[j].astype(F32))
            return carry

        lax.fori_loop(0, n, step, 0, unroll=min(4, n))

    def rs_copy(name, k):
        at = parts.index(name)
        size = sections >> (k + 1)
        if name == "dz":
            mate = sections_near[bits - 2 + k]
            src, dst = (stage.at[2:4, 0:tiles], phz[0]) if k == 0 else (stage.at[1, 0:tiles], phz[1])
        elif name[0] == "d":
            mate = inner.partner(k, sections_near, r)
            src, dst = stage.at[chunk_of(name), pl.ds(size, size)], phd[k].at[int(name[1])]
        else:
            mate = route_of[name].partner(k, sections_near, r)
            src, dst = stage.at[chunk_of(name), pl.ds(size, size)], pho[k].at[others.index(name)]
        return pltpu.make_async_remote_copy(
            src, dst, rs_send.at[at, k], rs_recv.at[at, k], device_id=(mate, r), device_id_type=MESH)

    def rs_step(name, k):
        if k > 0:
            rs_copy(name, k - 1).wait_recv()
        if name == "dz":
            if k == 1:
                for c in range(2):
                    add_blocks(c, phz[0].at[c], tiles)
            if k == 2:
                for q in range(tiles):
                    total = stage[0, q].astype(F32) + phz[1][q].astype(F32)
                    gdown[q * rb : (q + 1) * rb, pl.ds(aligned(half * r), half)] = total
        elif name[0] == "d":
            if k > 0:
                add_blocks(chunk_of(name), phd[k - 1].at[int(name[1])], sections >> k)
        elif k > 0:
            at = others.index(name)
            if k < bits:
                add_blocks(tiles + at, pho[k - 1].at[at], sections >> k)
            else:
                view = final_view(name)
                view[...] = stage[tiles + at, 0].astype(F32) + pho[k - 1][at, 0].astype(F32)
        if k < phases_of(name):
            rs_copy(name, k).start()
        elif name == "dz" or name[0] != "d":
            final_copy(name).start()

    def final_view(name):
        if name == "dz":
            return gdown.at[:, pl.ds(aligned(half * r), half)]
        out = {"u": gup, "o": gwout, "q": gqkv}[name[0]]
        c = int(name[1]) if len(name) > 1 else 0
        return out.at[:, pl.ds(aligned(c * width + half * r), half)]

    def final_copy(name):
        at = parts.index(name)
        return pltpu.make_async_remote_copy(
            final_view(name), final_view(name), f_send.at[at], f_recv.at[at], device_id=core, device_id_type=MESH)

    plan = PLAN if bits == 4 else later_plan(parts, phases_of)

    def at(point):
        for item in plan.get(point, ()):
            name, k = item.split(".")
            if name == "g":
                gain_step(int(k))
                continue
            if k == "0" and name != "dz":
                core_copy(name).wait()
                add_blocks(chunk_of(name), own_v.at[slot_of[name]], sections)
            rs_step(name, int(k))

    def gain_copy(k):
        mate = mates[k]
        return pltpu.make_async_remote_copy(
            gs.at[k], gr.at[k], gain_sem.at[0, k], gain_sem.at[1, k], device_id=mate, device_id_type=MESH)

    def gain_step(k):
        if k > 0:
            gain_copy(k - 1).wait_recv()
            gs[k] = gs[k - 1] + gr[k - 1]
        if k <= bits:
            gain_copy(k).start()
        else:
            gout[...] = gs[k]

    def do_copy(p):
        return pltpu.make_async_remote_copy(
            do_own.at[:, pl.ds(aligned(half * (1 - r)), half)], do_v.at[p, pl.ds(aligned(tokens * r, 16), tokens), :],
            do_sem.at[0, p], do_sem.at[1, p], device_id=core, device_id_type=MESH)

    def ds_copy(p, pair, sending):
        at = r if sending else 1 - r
        cols = pl.ds(aligned(half * at + PAIR * pair), PAIR)
        return pltpu.make_async_remote_copy(
            ds_tmp.at[pair, :, 1 - r], ds_v.at[:, pl.ds(p * tokens, tokens), cols], ds_send.at[p, pair],
            ds_recv.at[p, pair], device_id=core, device_id_type=MESH)

    def attention_pair(p, pair):
        off = aligned(pair * PAIR)
        cols = pl.ds(off, PAIR)
        blocks_of = [slice(i * tokens, (i + 1) * tokens) for i in range(2)]
        queries, grads = [], []
        for rows in blocks_of:
            q = qkv_v[p, 0, rows, cols]
            g = do_v[p, rows, cols]
            queries.append([q * mask for mask in masks])
            grads.append([g * mask for mask in masks])
        dq = [None, None]
        for src in range(p + 1):
            for j in range(2):
                at = blocks_of[j]
                key = qkv_v[src, 1, at, cols]
                value = qkv_v[src, 2, at, cols]
                keys = jnp.concatenate([key * mask for mask in masks], axis=0)
                probs, d_scores = [], []
                for i in range(j, 2):
                    for h in range(2):
                        lse = lse_v[p, 2 * pair + h, :, blocks_of[i]]
                        dd = dd_v[2 * pair + h, :, blocks_of[i]]
                        prob = jnp.exp(dot_nt(key, queries[i][h]) + bias[i + j].astype(F32) - lse)
                        d_prob = dot_nt(value, grads[i][h])
                        d_scores.append(low(prob * (d_prob - dd)))
                        probs.append(low(prob))
                    term = dot_tn(jnp.concatenate(d_scores[-2:], axis=0), keys)
                    dq[i] = term if dq[i] is None else dq[i] + term
                q_all = jnp.concatenate([v for i in range(j, 2) for v in queries[i]], axis=0)
                g_all = jnp.concatenate([v for i in range(j, 2) for v in grads[i]], axis=0)
                d_key = dot(jnp.concatenate(d_scores, axis=1), q_all)
                d_value = dot(jnp.concatenate(probs, axis=1), g_all)
                for kv, term in enumerate((d_key, d_value)):
                    if p == 1 and src == 0:
                        dkv0[kv, at, cols] = term.astype(dkv0.dtype)
                    else:
                        ds_tmp[pair, 1 + kv, j] = low(term if p == 1 else term + dkv0[kv, at, cols].astype(F32))
        for i in range(2):
            ds_tmp[pair, 0, i] = low(dq[i] * (HEAD ** -0.5))
        mine = pl.ds(aligned(half * r + off), PAIR)
        for c in range(3):
            ds_v[c, pl.ds(p * tokens, tokens), mine] = ds_tmp[pair, c, r]
        ds_copy(p, pair, True).start()

    def sg_own_copy():
        return pltpu.make_async_copy(dm_v, sgrad.at[0, m], sg_local.at[0])

    head_row = lax.broadcasted_iota(jnp.int32, (16, half), 0)
    head_of = lax.broadcasted_iota(jnp.int32, (16, half), 1)
    picks = low(jnp.where((head_of >= head_row * HEAD) & (head_of < (head_row + 1) * HEAD), 1.0, 0.0))

    own_pass.wait()
    other_pass.wait()

    for p in (1, 0):
        if p == 0:
            def join(rows):
                total = df_v[0, rows, :].astype(F32) + low(dm_v[rows, :]).astype(F32)
                dn_v[rows, :] = total
                df_v[0, rows, :] = low(total)

            by_rows(tokens, join)
            ld_gp0.wait()
            ld_g.wait()
            at("join")
            for t in range(tiles):
                put_tile(f"d{t}", lambda at, n: g_v[:, :, t * width + at : t * width + at + n].reshape(2 * tokens, n),
                         df_v[...].reshape(2 * tokens, width))
                at(f"wd{t}")
        for t, cols in enumerate(blocks):
            if p == 1:
                ld_first[t][0].wait()
                ld_first[t][1].wait()
            dg = dot_nt(df_v[p], wdown_v[cols, :])
            du_v[p, :, cols] = low(dg * du_v[p, :, cols].astype(F32))
        if p == 1:
            ld_up.wait()
            ld_m1.wait()
            ld_out = load(wout, wout_v, 6)
            ld_qkv = load(qkv_i, qkv_v, 7)
            ld_o32 = load(o32_i.at[1], o32_v, 8)
            ld_lse = load(lse_i, lse_v, 9)
        else:
            ld_o = load(o_i, df_v, 15)
            ld_m0.wait()

            @pl.when(m == 1)
            def _():
                sg_own_copy().wait()

            at("units")
            ld_b.wait()
            for t in range(tiles):
                put_tile(f"u{t}", lambda at, n: b_v[:, :, at : at + n].reshape(2 * tokens, n),
                         du_v[:, :, t * width : (t + 1) * width].reshape(2 * tokens, width))
                at(f"wu{t}")
            ld_a = load(a_i, b_v, 16)
        dm_v[...] = dot_nt(du_v[p], wup_v[...])
        if p == 0:
            at("db")

        def norm_two_back(rows):
            xh, scale = norm_parts(m_v[rows, :])
            dy = dm_v[rows, :]
            gs[0, 1:2, :] += jnp.sum(dy * xh, axis=0, keepdims=True)
            dxh = dy * gain2
            dv = scale * (dxh - mean_of(dxh) - xh * mean_of(dxh * xh))
            grad = df_v[1, rows, :].astype(F32) if p == 1 else dn_v[rows, :]
            total = grad + dv
            dm_v[rows, :] = total
            dc_v[p, rows, :] = low(total)

        by_rows(tokens, norm_two_back)
        ld_x = load(x_i.at[p], m_v, 11 + p)
        if p == 1:
            ld_out.wait()
            ld_wqkv = load(wqkv, wqkv_v, 10)
        else:
            at("ln2")
            do_copy(1).wait_send()
        do_own[...] = low(dot_nt(dc_v[p], wout_v[...]))
        do_copy(p).start()
        do_v[p, pl.ds(aligned(tokens * r, 16), tokens), :] = do_own[:, pl.ds(aligned(half * r), half)]
        if p == 1:
            ld_qkv.wait()
            ld_lse.wait()
            ld_o32.wait()
            ld_gp0 = load(gp_i.at[0], du_v.at[0], 18)
            hid_own.wait()
            hid_out = pltpu.make_async_copy(sg_send_v, hidden.at[0, m], in_sem.at[5])
            hid_out.start()
            ld_g = load(g_i, g_v, 13)
            ld_b = load(b_i, b_v, 14)
        else:
            at("do")
            ld_o320.wait()
        do_copy(p).wait_recv()
        for i in range(2):
            rows = slice(i * tokens, (i + 1) * tokens)
            prod = do_v[p, rows, :].astype(F32) * o32_v[rows, :]
            upper = low(prod)
            rest = low(prod - upper.astype(F32))
            sums = dot_nt(picks, upper) + dot_nt(picks, rest)
            for h in range(2 * pairs):
                dd_v[h, :, rows] = sums[h : h + 1, :]
        if p == 1:
            ld_o320 = load(o32_i.at[0], o32_v, 20)

            def pair_step(pair, carry):
                attention_pair(1, pair)
                return carry

            lax.fori_loop(0, pairs, pair_step, 0)
        else:
            at("dowait")
            for pair in range(pairs):
                ds_copy(1, pair, True).wait_send()
            for pair in range(pairs):
                attention_pair(0, pair)
                at(f"at{pair}")
            ld_o.wait()
            put_tile("o", lambda at, n: df_v[:, :, at : at + n].reshape(2 * tokens, n), dc_v[...].reshape(2 * tokens, width))
            at("wo")
            ld_a.wait()
        for pair in range(pairs):
            ds_copy(p, pair, False).wait_recv()
        if p == 1:
            ld_wqkv.wait()
        else:
            at("dswait")
            for c in range(3):
                put_tile(f"q{c}", lambda at, n: b_v[:, :, at : at + n].reshape(2 * tokens, n), ds_v[c])
                at(f"wq{c}")
        ld_x.wait()
        for c in range(3):
            term = dot_nt(ds_v[c, p * tokens : (p + 1) * tokens, :], wqkv_v[:, c * width : (c + 1) * width])
            dn_v[...] = term if c == 0 else dn_v[...] + term
        if p == 0:
            at("da")

        def norm_one_back(rows):
            xh, scale = norm_parts(m_v[rows, :])
            dy = dn_v[rows, :]
            gs[0, 0:1, :] += jnp.sum(dy * xh, axis=0, keepdims=True)
            dxh = dy * gain1
            dv = scale * (dxh - mean_of(dxh) - xh * mean_of(dxh * xh))
            dm_v[rows, :] = dm_v[rows, :] + dv

        by_rows(tokens, norm_one_back)

        if p == 1:
            hid_out.wait()

        @pl.when(m == p)
        def _():
            sg_own_copy().start()

        @pl.when(m != p)
        def _():
            sg_send_v[...] = low(dm_v[...])
            pltpu.make_async_remote_copy(
                sg_send_v, sg_recv_v, sg_sem.at[0], sg_sem.at[1], device_id=relay, device_id_type=MESH).start()

        if p == 1:
            ld_m0 = load(m_i.at[0], m_v, 19)

    gain_step(0)
    at("ln1")
    at("end")
    sg_copy = pltpu.make_async_remote_copy(
        sg_send_v, sg_recv_v, sg_sem.at[0], sg_sem.at[1], device_id=relay, device_id_type=MESH)
    sg_copy.wait_recv()
    dn_v[...] = sg_recv_v[...].astype(F32)
    sg_last = pltpu.make_async_copy(dn_v, sgrad.at[0, 1 - m], sg_local.at[1])
    sg_last.start()

    for name in parts:
        if name == "dz" or name[0] != "d":
            final_copy(name).wait()
        for k in range(phases_of(name)):
            rs_copy(name, k).wait_send()
    hid_copy.wait()
    for k in range(bits + 1):
        gain_copy(k).wait_send()
    do_copy(0).wait_send()
    for pair in range(pairs):
        ds_copy(0, pair, True).wait_send()
    sg_copy.wait_send()

    @pl.when(m == 0)
    def _():
        sg_own_copy().wait()

    sg_last.wait()


def shape(dims, dtype):
    return jax.ShapeDtypeStruct(dims, dtype)


def forward_call(stream, cot, seg, gains, weights):
    wqkv, wout, wup, wdown = weights
    _, _, tokens, width = stream.shape
    units = wup.shape[1]
    half = width // 2
    length = 2 * tokens
    pairs = half // PAIR
    saved = [
        shape((2, tokens, width), F32),
        shape((2, tokens, width), BF16),
        shape((2, 3, length, half), BF16),
        shape((2, length, half), F32),
        shape((2, tokens, width), BF16),
        shape((2, tokens, width), F32),
        shape((2, tokens, width), BF16),
        shape((2, tokens, units), BF16),
        shape((2, tokens, units), BF16),
        shape((2, 2 * pairs, 1, length), F32),
    ]
    anyspace = pl.BlockSpec(memory_space=pl.ANY)
    vmem = pl.BlockSpec(memory_space=pltpu.VMEM)
    V = pltpu.VMEM
    sem = pltpu.SemaphoreType.DMA
    return pl.pallas_call(
        forward_kernel,
        out_shape=[shape((2, tokens, width), BF16), shape((tokens, width), BF16)] + saved,
        in_specs=[anyspace, anyspace, vmem, vmem, vmem] + [anyspace] * 4,
        out_specs=[anyspace] * 12,
        scratch_shapes=[
            V(wqkv.shape, BF16), V(wout.shape, BF16), V(wup.shape, BF16), V(wdown.shape, BF16),
            V((tokens, width), BF16), V((tokens, width), BF16), V((2, tokens, width), F32),
            V((2, tokens, width), BF16), V((2, 3, tokens, width), BF16), V((2, 3, length, half), BF16),
            V((2, length, half), F32), V((2, pairs, 2, tokens, PAIR), BF16), V((2, tokens, width), BF16),
            V((2, tokens, width), F32), V((2, tokens, width), BF16), V((2, tokens, units), BF16),
            V((2, tokens, units), BF16), V((tokens, width), F32), V((2, tokens, width), BF16),
            V((2, 2 * pairs, 1, length), F32), V((3, tokens, tokens), F32),
            sem((5,)), sem((2 * (9 + 2 * (units // width)),)), sem((2,)), sem((2,)),
            sem((2, 3)), sem((2, 3)), sem((2, pairs)), sem((2, pairs)),
        ],
        compiler_params=pltpu.CompilerParams(collective_id=0, has_side_effects=True, vmem_limit_bytes=VMEM_LIMIT),
        name="forward",
    )(stream, cot, seg, *gains, wqkv, wout, wup, wdown)


def backward_call(hid, cot, cotx, seg, gains, weights, saved, sections):
    wqkv, wout, wup, wdown = weights
    _, _, tokens, width = cot.shape
    units = wup.shape[1]
    half = width // 2
    length = 2 * tokens
    pairs = half // PAIR
    tiles = units // width
    chunks = 2 * tiles + 4
    bits = sections.bit_length() - 1
    assert 2 ** bits == sections and bits >= 4 and tiles == 4
    rb = width // sections
    spare = F32 if rb % 16 == 0 else BF16
    anyspace = pl.BlockSpec(memory_space=pl.ANY)
    vmem = pl.BlockSpec(memory_space=pltpu.VMEM)
    V = pltpu.VMEM
    sem = pltpu.SemaphoreType.DMA

    def body(*refs):
        fixed = len(scratch) + 20 + 7
        phd, refs_z = refs[fixed : fixed + bits - 2], refs[fixed + bits - 2 :]
        phz, pho, rest = refs_z[:2], refs_z[2 : 2 + bits], refs_z[2 + bits :]
        backward_kernel(bits, *refs[:fixed], phd, phz, pho, *rest)

    scratch = [
        V(wqkv.shape, BF16), V(wout.shape, BF16), V(wup.shape, BF16), V(wdown.shape, BF16),
        V((tokens, width), F32), V((length, half), F32),
        V((2, 3, length, half), BF16), V((2, 2 * pairs, 1, length), F32),
        V((2, tokens, width), BF16), V((2, tokens, units), BF16),
        V((2, tokens, width), BF16), V((2, tokens, units), BF16), V((2, tokens, width), BF16),
        V((3, 2 * tokens, width), BF16), V((tokens, width), BF16), V((2, length, half), BF16),
        V((2 * pairs, 1, length), F32), V((tokens, width), F32), V((tokens, width), F32),
        V((3, tokens, tokens), spare), V((2, length, half), spare),
        V((pairs, 3, 2, tokens, PAIR), BF16),
        V((tokens, width), BF16), V((tokens, width), BF16),
        V((width // 2, width), F32), V((tiles, sections, rb, half), BF16), V((tiles, sections, rb, half), BF16),
        V((chunks, sections, rb, half), BF16),
    ]
    ph = [V((tiles, sections >> (k + 1), rb, half), BF16) for k in range(bits - 2)]
    ph += [V((2, tiles, rb, half), BF16), V((tiles, rb, half), BF16)]
    ph += [V((chunks - tiles, sections >> (k + 1), rb, half), BF16) for k in range(bits)]
    rest = [
        V((bits + 2, 8, width), F32), V((bits + 1, 8, width), F32),
        sem((21 + 2 * tiles,)), sem((2,)), sem((2,)), sem((2,)), sem((2, 2)), sem((2, pairs)), sem((2, pairs)),
        sem((chunks + 1,)), sem((chunks + 1,)), sem((chunks + 1, bits)), sem((chunks + 1, bits)),
        sem((chunks + 1,)), sem((chunks + 1,)), sem((2, bits + 1)),
    ]
    return pl.pallas_call(
        body,
        out_shape=[
            shape(cot.shape, BF16), shape(cot.shape, F32), shape((8, width), F32), shape((rb, 3 * width), F32), shape((rb, width), F32),
            shape((rb, units), F32), shape((tiles * rb, width), F32),
        ],
        in_specs=[anyspace, anyspace, anyspace, vmem, vmem, vmem] + [anyspace] * 14,
        out_specs=[anyspace] * 2 + [vmem] * 5,
        scratch_shapes=scratch + ph + rest,
        compiler_params=pltpu.CompilerParams(collective_id=1, has_side_effects=True, vmem_limit_bytes=VMEM_LIMIT),
        name="backward",
    )(hid, cot, cotx, seg, *gains, wqkv, wout, wup, wdown, *saved)


def finish_kernel(sections, gout, *refs):
    n = (len(refs) - 3) // 3
    sources, targets, gain1, gain2 = refs[:n], refs[n : 2 * n], refs[2 * n], refs[2 * n + 1]
    held, sem = refs[2 * n + 2 : -1], refs[-1]
    ins = [pltpu.make_async_copy(a, b, sem.at[0, i]) for i, (a, b) in enumerate(zip(sources, held))]
    outs = [pltpu.make_async_copy(a, b, sem.at[1, i]) for i, (a, b) in enumerate(zip(held, targets))]
    for copy in ins:
        copy.start()
    width = gout.shape[1]
    rb = width // sections
    s = lax.axis_index("section")
    turned = pltpu.roll(gout[...], lax.rem(width - s * rb, width), 1)
    gain1[...] = turned[0, :rb]
    gain2[...] = turned[1, :rb]
    for arrived, copy in zip(ins, outs):
        arrived.wait()
        copy.start()
    for copy in outs:
        copy.wait()


def finish_call(gout, arrays, sections):
    anyspace = pl.BlockSpec(memory_space=pl.ANY)
    vmem = pl.BlockSpec(memory_space=pltpu.VMEM)
    gain = shape((gout.shape[1] // sections,), F32)
    return pl.pallas_call(
        functools.partial(finish_kernel, sections),
        out_shape=[shape(a.shape, a.dtype) for a in arrays] + [gain, gain],
        in_specs=[vmem] + [anyspace] * len(arrays),
        out_specs=[anyspace] * len(arrays) + [vmem, vmem],
        scratch_shapes=[pltpu.VMEM(a.shape, a.dtype) for a in arrays] + [pltpu.SemaphoreType.DMA((2, len(arrays)))],
        compiler_params=pltpu.CompilerParams(vmem_limit_bytes=VMEM_LIMIT),
        name="finish",
    )(gout, *arrays)


def per_device(stream, segment_ids, ln1_gain, w_qkv, w_out, ln2_gain, w_up, w_down, cotangent):
    sections = lax.axis_size("section")
    gains = (ln1_gain, ln2_gain)
    weights = (w_qkv, w_out, w_up, w_down)
    hid, cotx, *saved = forward_call(stream, cotangent, segment_ids, gains, weights)
    hidden, sgrad, gout, gqkv, gwout, gup, gdown = backward_call(hid, cotangent, cotx, segment_ids, gains, weights, saved, sections)
    hidden, sgrad, gqkv, gwout, gup, gdown, gain1, gain2 = finish_call(
        gout, (hidden, sgrad, gqkv, gwout, gup, gdown), sections)
    return (hidden, sgrad, gain1, gqkv, gwout, gain2, gup, gdown)


def solution(mesh):
    rows = P("section", None, "rows", None)
    assert mesh.shape["rows"] == 2
    return jax.shard_map(
        per_device,
        mesh=mesh,
        in_specs=(rows, P("section", None, None), P(), P(), P(), P(), P(), P(), rows),
        out_specs=(rows, rows, P("section"), P("section", None), P("section", None), P("section"),
                   P("section", None), P("section", None)),
        check_vma=False,
    )
```

```python
import functools

import jax
import jax.numpy as jnp
from jax import lax
from jax.experimental import pallas as pl
from jax.experimental.pallas import tpu as pltpu
from jax.sharding import PartitionSpec as P

HEAD = 64
PAIR = 128
EPS = 1e-05
MASKED = -1e30
F32 = jnp.float32
BF16 = jnp.bfloat16
MESH = pl.DeviceIdType.MESH
GELU_A = 0.7978845608
GELU_B = 0.044715
CHUNK = 64
VMEM_LIMIT = 65300 * 1024


def dot(a, b):
    return jnp.dot(a, b, preferred_element_type=F32)


def dot_nt(a, b):
    return lax.dot_general(a, b, (((1,), (1,)), ((), ())), preferred_element_type=F32)


def dot_tn(a, b):
    return lax.dot_general(a, b, (((0,), (0,)), ((), ())), preferred_element_type=F32)


def low(v):
    return v.astype(BF16)


def mean_of(v):
    return jnp.sum(v, axis=-1, keepdims=True) * (1.0 / v.shape[-1])


def norm_parts(v):
    centered = v - mean_of(v)
    scale = lax.rsqrt(mean_of(centered * centered) + EPS)
    return centered * scale, scale


def by_rows(rows, body):
    def step(i, carry):
        body(pl.ds(pl.multiple_of(i * CHUNK, CHUNK), CHUNK))
        return carry

    lax.fori_loop(0, rows // CHUNK, step, 0, unroll=True)


def place():
    r = lax.axis_index("rows")
    s = lax.axis_index("section")
    m = lax.rem(s, 2)
    return r, s, m


def aligned(value, unit=128):
    return value if isinstance(value, int) else pl.multiple_of(value, unit)


def head_masks():
    lane = lax.broadcasted_iota(jnp.int32, (1, PAIR), 1)
    first = jnp.where(lane < HEAD, 1.0, 0.0)
    return low(first), low(1.0 - first)


def fill_bias(seg_ref, m, bias, tokens):
    length = 2 * tokens
    row = seg_ref[0, pl.ds(m, 1), :].astype(F32)
    col = jnp.broadcast_to(row, (PAIR, length)).T
    key_at = lax.broadcasted_iota(jnp.int32, (tokens, tokens), 0)
    query_at = lax.broadcasted_iota(jnp.int32, (tokens, tokens), 1)
    for i, j in ((0, 0), (1, 0), (1, 1)):
        seen = col[j * tokens : (j + 1) * tokens, :1] == row[:, i * tokens : (i + 1) * tokens]
        if i == j:
            seen = seen & (key_at <= query_at)
        bias[i + j] = jnp.where(seen, 0.0, MASKED).astype(bias.dtype)


def forward_kernel(
    stream, cot, seg, gain1_ref, gain2_ref, wqkv, wout, wup, wdown,
    hid_o, cotx, x_o, a_o, qkv_o, o32_o, o_o, m_o, b_o, g_o, gp_o, lse_o,
    wqkv_v, wout_v, wup_v, wdown_v, e_own, e_recv, x_v, a_v, own_qkv, qkv_v, o32_v, o_tmp, o_v,
    m_v, b_v, g_v, gp_v, h_v, hid_v, lse_v, bias,
    in_sem, out_sem, e_sem, cot_sem, q_send, q_recv, o_send, o_recv,
):
    r, s, m = place()
    tokens, width = e_own.shape
    half = width // 2
    hidden_units = wup_v.shape[1]
    pairs = half // PAIR
    core = (s, 1 - r)
    relay = (s + 1 - 2 * m, r)

    loads = [
        pltpu.make_async_copy(stream.at[0, m], e_own, in_sem.at[0]),
        pltpu.make_async_copy(wqkv, wqkv_v, in_sem.at[1]),
        pltpu.make_async_copy(wout, wout_v, in_sem.at[2]),
        pltpu.make_async_copy(wup, wup_v, in_sem.at[3]),
        pltpu.make_async_copy(wdown, wdown_v, in_sem.at[4]),
    ]
    barrier = pltpu.get_barrier_semaphore()
    pl.semaphore_signal(barrier, inc=1, device_id=core, device_id_type=MESH)
    pl.semaphore_signal(barrier, inc=1, device_id=relay, device_id_type=MESH)
    for load in loads:
        load.start()
    pl.semaphore_wait(barrier, 2)

    halves = [slice(0, tokens // 2), slice(tokens // 2, tokens)]
    e_copies = [
        pltpu.make_async_remote_copy(
            stream.at[0, 1 - m, rows], e_recv.at[rows], e_sem.at[0, i], e_sem.at[1, i],
            device_id=relay, device_id_type=MESH)
        for i, rows in enumerate(halves)]
    for copy in e_copies:
        copy.start()
    cot_copy = pltpu.make_async_remote_copy(
        cot.at[0, 1 - m], cotx, cot_sem.at[0], cot_sem.at[1], device_id=relay, device_id_type=MESH)

    fill_bias(seg, m, bias, tokens)
    masks = head_masks()
    stores = []

    def store(src, dst):
        copy = pltpu.make_async_copy(src, dst, out_sem.at[len(stores)])
        copy.start()
        stores.append(copy)

    def attention(p):
        lane = lax.broadcasted_iota(jnp.int32, (tokens, PAIR), 1)

        def pair_step(pair, carry):
            off = aligned(pair * PAIR)
            cols = pl.ds(off, PAIR)
            for i in range(2):
                rows = slice(i * tokens, (i + 1) * tokens)
                q = qkv_v[p, 0, rows, cols]
                mixed = []
                for h in range(2):
                    q_h = q * masks[h]
                    scores, values = [], []
                    for src in range(p + 1):
                        for j in range(i + 1):
                            at = slice(j * tokens, (j + 1) * tokens)
                            scores.append(dot_nt(qkv_v[src, 1, at, cols], q_h) + bias[i + j])
                            values.append((src, at))
                    top = jnp.max(functools.reduce(jnp.maximum, scores), axis=0, keepdims=True)
                    expo = [jnp.exp(z - top) for z in scores]
                    total = jnp.sum(functools.reduce(jnp.add, expo), axis=0, keepdims=True)
                    share = 1.0 / total
                    probs = jnp.concatenate([low(e * share) for e in expo], axis=0)
                    seen = jnp.concatenate([qkv_v[src, 2, at, cols] for src, at in values], axis=0)
                    mixed.append(dot_tn(probs, seen))
                    lse_v[p, 2 * pair + h, :, rows] = top + jnp.log(total)
                both = jnp.where(lane < HEAD, mixed[0], mixed[1])
                o32_v[p, rows, cols] = both
                o_tmp[p, pair, i] = low(both)
            mine = pl.ds(aligned(half * r + off), PAIR)
            o_v[p, :, mine] = o_tmp[p, pair, r]
            pltpu.make_async_remote_copy(
                o_tmp.at[p, pair, 1 - r], o_v.at[p, :, mine], o_send.at[p, pair], o_recv.at[p, pair],
                device_id=core, device_id_type=MESH).start()
            return carry

        for pair in range(pairs):
            pair_step(pair, 0)

    def o_copy(p, pair):
        cols = pl.ds(aligned(half * (1 - r) + PAIR * pair), PAIR)
        return pltpu.make_async_remote_copy(
            o_tmp.at[p, pair, r], o_v.at[p, :, cols], o_send.at[p, pair], o_recv.at[p, pair],
            device_id=core, device_id_type=MESH)

    gain1 = gain1_ref[...].astype(F32).reshape(1, width)
    gain2 = gain2_ref[...].astype(F32).reshape(1, width)

    for p in range(2):
        if p == 0:
            loads[0].wait()
        else:
            @pl.when(m == 0)
            def _():
                for copy in e_copies:
                    copy.wait_recv()
                x_v[1] = hid_v[0].astype(F32) + e_recv[...].astype(F32)

            @pl.when(m == 1)
            def _():
                x_v[1] = hid_v[0].astype(F32) + e_own[...].astype(F32)

        q_copies = []
        pieces = halves if p == 0 else [slice(0, tokens)]
        for at, piece in enumerate(pieces):
            if p == 0:
                @pl.when(m == 0)
                def _():
                    x_v[0, piece, :] = e_own[piece, :].astype(F32)

                @pl.when(m == 1)
                def _():
                    e_copies[at].wait_recv()
                    x_v[0, piece, :] = e_recv[piece, :].astype(F32)

            for first in range(piece.start, piece.stop, CHUNK):
                rows = slice(first, first + CHUNK)
                xh, _ = norm_parts(x_v[p, rows, :])
                a_v[p, rows, :] = low(xh * gain1)
            if p == 0 and at == 0:
                loads[1].wait()
            for c in range(3):
                part = low(dot(a_v[p, piece, :], wqkv_v[:, c * width : (c + 1) * width]))
                if c == 0:
                    part = part * low(jnp.full((1, 1), HEAD ** -0.5, F32))
                own_qkv[p, c, piece, :] = part
                if piece.stop == tokens:
                    their = pl.ds(aligned(half * (1 - r)), half)
                    copy = pltpu.make_async_remote_copy(
                        own_qkv.at[p, c, :, their], qkv_v.at[p, c, pl.ds(aligned(tokens * r, 16), tokens), :],
                        q_send.at[p, c], q_recv.at[p, c], device_id=core, device_id_type=MESH)
                    copy.start()
                    q_copies.append(copy)
        for c in range(3):
            qkv_v[p, c, pl.ds(aligned(tokens * r, 16), tokens), :] = own_qkv[p, c, :, pl.ds(aligned(half * r), half)]
        store(x_v.at[p], x_o.at[p])
        store(a_v.at[p], a_o.at[p])
        for copy in q_copies:
            copy.wait_recv()
        attention(p)
        store(qkv_v.at[p], qkv_o.at[p])
        store(o32_v.at[p], o32_o.at[p])
        store(lse_v.at[p], lse_o.at[p])
        if p == 0:
            loads[2].wait()
            for copy in e_copies:
                copy.wait_send()
            cot_copy.start()
        for pair in range(pairs):
            o_copy(p, pair).wait_recv()
        m_v[p] = x_v[p] + dot(o_v[p], wout_v[...])

        def norm_two(rows):
            xh, _ = norm_parts(m_v[p, rows, :])
            b_v[p, rows, :] = low(xh * gain2)

        by_rows(tokens, norm_two)
        store(o_v.at[p], o_o.at[p])
        store(m_v.at[p], m_o.at[p])
        store(b_v.at[p], b_o.at[p])
        if p == 0:
            loads[3].wait()
            loads[4].wait()
        h_v[...] = m_v[p]

        for t in range(hidden_units // width):
            cols = slice(t * width, (t + 1) * width)
            u = dot(b_v[p], wup_v[:, cols])
            squared = u * u
            tan = jnp.tanh(u * (GELU_A + (GELU_A * GELU_B) * squared))
            upper = 0.5 + 0.5 * tan
            g_v[p, :, cols] = low(u * upper)
            slope = (0.5 * u) * (1.0 - tan * tan) * (GELU_A + (3.0 * GELU_A * GELU_B) * squared)
            gp_v[p, :, cols] = low(upper + slope)
            store(g_v.at[p, :, cols], g_o.at[p, :, cols])
            store(gp_v.at[p, :, cols], gp_o.at[p, :, cols])
            if t > 0:
                before = slice((t - 1) * width, t * width)
                h_v[...] += dot(g_v[p, :, before], wdown_v[before, :])
        h_v[...] += dot(g_v[p, :, hidden_units - width :], wdown_v[hidden_units - width :, :])
        hid_v[p] = low(h_v[...])
        store(hid_v.at[p], hid_o.at[p])

    cot_copy.wait()
    for p in range(2):
        for c in range(3):
            pltpu.make_async_remote_copy(
                own_qkv.at[p, c, :, pl.ds(aligned(half * (1 - r)), half)],
                qkv_v.at[p, c, pl.ds(aligned(tokens * r, 16), tokens), :],
                q_send.at[p, c], q_recv.at[p, c], device_id=core, device_id_type=MESH).wait_send()
        for pair in range(pairs):
            o_copy(p, pair).wait_send()
    for copy in stores:
        copy.wait()


class Route:
    def __init__(self, bits, late):
        self.bits = bits
        self.late = late

    def weights(self, r):
        n = self.bits
        if self.late:
            low_unit, rest = 1, [2 ** (n + 1 - b) for b in range(2, n)]
        else:
            low_unit, rest = 2 ** (n - 2), [2 ** (n - 1 - b) for b in range(2, n)]
        return [low_unit * (2 - r), low_unit * (1 + r)] + rest

    def slot(self, s_bits, my_bits, weights):
        total = 0
        for a, b, w in zip(s_bits, my_bits, weights):
            total = total + w * (1 - b if a else b)
        return total

    def partner(self, k, mates, r):
        n = self.bits
        at = k + 2 if self.late else k
        if self.late and k >= n - 2:
            at = k - (n - 2)
        if at > 1:
            return mates[at]
        return mates[at] + r * (mates[1 - at] - mates[at])


START = {
    "wd2": ("d0.0",), "wd3": ("d1.0",), "units": ("d2.0", "d3.0"), "wu2": ("u0.0",), "wu3": ("u1.0",), "db": ("u2.0",),
    "ln2": ("u3.0",), "dswait": ("o.0",), "wq2": ("q0.0",), "da": ("q1.0", "q2.0"),
}
PLAN = {
    "wd3": ("d2.0", "d0.0", "d1.0", "d3.0"),
    "wu1": ("u0.0",),
    "do": ("u1.0", "u2.0", "d0.1", "d1.1"),
    "dowait": ("u3.0", "d2.1"),
    "at0": ("d3.1", "u0.1"),
    "at2": ("d1.2", "d0.2", "d2.2", "u1.1", "d3.2", "u3.1"),
    "wo": ("dz.0", "u2.1"),
    "dswait": ("o.0",),
    "wq1": ("u0.2", "q0.0"),
    "da": ("u2.2", "u1.2", "q1.0", "dz.1", "u3.2", "o.1", "q2.0", "u3.3", "u0.3"),
    "ln1": ("u1.3", "g.1"),
    "end": ("q0.1", "q1.1", "dz.2", "o.2", "g.2", "u2.3", "u1.4", "u3.4", "q2.1", "g.3", "q0.2", "u0.4",
        "o.3", "q1.2", "g.4", "q2.2", "q0.3", "q1.3", "q2.3", "g.5", "q0.4", "o.4", "u2.4", "q1.4",
        "q2.4"),
}


def later_plan(parts, phases_of):
    low_parts = [n for n in parts if n[0] == "d" and n != "dz"]
    rest = [n for n in parts if n[0] != "d"]
    steps = [f"{n}.{k}" for k in range(1, phases_of("d0") + 1) for n in low_parts] + ["dz.0", "dz.1", "dz.2"]
    for k in range(1, phases_of("o") + 1):
        steps += [f"g.{k}"] + [f"{n}.{k}" for n in rest]
    return START | {"end": steps + [f"g.{phases_of('o') + 1}"]}


def backward_kernel(
    bits,
    hid_i, cot, cotx, seg, gain1_ref, gain2_ref, wqkv, wout, wup, wdown, x_i, a_i, qkv_i, o32_i, o_i, m_i, b_i, g_i, gp_i, lse_i,
    hidden, sgrad, gout, gqkv, gwout, gup, gdown,
    wqkv_v, wout_v, wup_v, wdown_v, m_v, o32_v, qkv_v, lse_v, b_v, g_v,
    df_v, du_v, dc_v, ds_v, do_own, do_v, dd_v, dm_v, dn_v, bias, dkv0, ds_tmp,
    sg_send_v, sg_recv_v,
    tile, send_v, own_v, stage, phd, phz, pho, gs, gr,
    in_sem, hid_sem, sg_sem, sg_local, do_sem, ds_send, ds_recv, c_send, c_recv, rs_send, rs_recv, f_send, f_recv, gain_sem,
):
    r, s, m = place()
    tokens, width = df_v.shape[1:]
    half = width // 2
    hidden_units = wup_v.shape[1]
    tiles = hidden_units // width
    pairs = half // PAIR
    sections = 2 ** bits
    rb = width // sections
    core = (s, 1 - r)
    relay = (s + 1 - 2 * m, r)
    n_in = 0

    def load(src, dst, at):
        copy = pltpu.make_async_copy(src, dst, in_sem.at[at])
        copy.start()
        return copy

    my_bits = [lax.rem(lax.div(s, 2 ** b), 2) for b in range(bits)]
    sections_near = [s + (1 - 2 * my_bits[b]) * 2 ** b for b in range(bits)]
    barrier = pltpu.get_barrier_semaphore()
    mates = [core]
    for b in range(bits):
        mates.append((sections_near[b], r))
    for mate in mates:
        pl.semaphore_signal(barrier, inc=1, device_id=mate, device_id_type=MESH)

    own_pass = load(cot.at[0, m], df_v.at[m], 0)
    other_pass = load(cotx, df_v.at[1 - m], 1)
    blocks = [pl.ds(t * width, width) for t in range(tiles)]
    ld_first = [(load(wdown.at[b, :], wdown_v.at[b, :], 21 + 2 * t), load(gp_i.at[1, :, b], du_v.at[1, :, b], 22 + 2 * t))
                for t, b in enumerate(blocks)]
    ld_up = load(wup, wup_v, 4)
    ld_m1 = load(m_i.at[1], m_v, 17)
    fill_bias(seg, m, bias, tokens)
    masks = head_masks()
    gain1 = gain1_ref[...].astype(F32).reshape(1, width)
    gain2 = gain2_ref[...].astype(F32).reshape(1, width)
    gs[0] = jnp.zeros(gs.shape[1:], F32)
    pl.semaphore_wait(barrier, len(mates))
    hid_own = load(hid_i.at[m], sg_send_v, 5)
    hid_copy = pltpu.make_async_remote_copy(
        hid_i.at[1 - m], hidden.at[0, m], hid_sem.at[0], hid_sem.at[1], device_id=relay, device_id_type=MESH)
    hid_copy.start()

    near = Route(bits, False)
    far = Route(bits, True)
    inner = Route(bits - 2, False)
    weights_of = {(route, who): route.weights(r if who else 1 - r) for route in (near, far, inner) for who in (0, 1)}
    others = [f"u{t}" for t in range(tiles)] + ["o", "q0", "q1", "q2"]
    route_of = {name: far if name in ("u0", "u1",) else near for name in others}
    parts = [f"d{t}" for t in range(tiles)] + ["dz"] + others
    slot_of = {f"d{t}": t for t in range(tiles)} | {f"u{t}": t for t in range(tiles)} | {"o": 0, "q0": 1, "q1": 2, "q2": 3}

    def tile_place(t):
        low_bit, high_bit = my_bits[bits - 2], my_bits[bits - 1]
        return 2 * (1 - low_bit if t & 1 else low_bit) + (1 - high_bit if t >> 1 else high_bit)

    def chunk_of(name):
        return tile_place(int(name[1])) if name[0] == "d" else tiles + others.index(name)

    def phases_of(name):
        return 2 if name == "dz" else bits - 2 if name[0] == "d" else bits

    def place_of(name, b, who):
        if name[0] == "d":
            bits_of = [((b // tiles) >> k) & 1 for k in range(bits - 2)]
            return inner.slot(bits_of, my_bits, weights_of[inner, who]) * tiles + b % tiles
        route = route_of[name]
        return route.slot([(b >> k) & 1 for k in range(bits)], my_bits, weights_of[route, who])

    def put_tile(name, lhs, rhs):
        part = width // 2
        slot = slot_of[name]
        for piece in range(2):
            tile[...] = dot_tn(lhs(piece * part, part), rhs)
            for bb in range(sections // 2):
                b = piece * (sections // 2) + bb
                theirs, mine = place_of(name, b, 0), place_of(name, b, 1)
                rows = slice(bb * rb, (bb + 1) * rb)
                send_v[slot, theirs] = low(tile[rows, pl.ds(aligned(half * (1 - r)), half)])
                own_v[slot, mine] = low(tile[rows, pl.ds(aligned(half * r), half)])
        core_copy(name).start()

    def core_copy(name):
        at = parts.index(name)
        return pltpu.make_async_remote_copy(
            send_v.at[slot_of[name]], stage.at[chunk_of(name)], c_send.at[at], c_recv.at[at],
            device_id=core, device_id_type=MESH)

    def add_blocks(c, other, n):
        def step(j, carry):
            stage[c, j] = low(stage[c, j].astype(F32) + other[j].astype(F32))
            return carry

        lax.fori_loop(0, n, step, 0, unroll=min(4, n))

    def rs_copy(name, k):
        at = parts.index(name)
        size = sections >> (k + 1)
        if name == "dz":
            mate = sections_near[bits - 2 + k]
            src, dst = (stage.at[2:4, 0:tiles], phz[0]) if k == 0 else (stage.at[1, 0:tiles], phz[1])
        elif name[0] == "d":
            mate = inner.partner(k, sections_near, r)
            src, dst = stage.at[chunk_of(name), pl.ds(size, size)], phd[k].at[int(name[1])]
        else:
            mate = route_of[name].partner(k, sections_near, r)
            src, dst = stage.at[chunk_of(name), pl.ds(size, size)], pho[k].at[others.index(name)]
        return pltpu.make_async_remote_copy(
            src, dst, rs_send.at[at, k], rs_recv.at[at, k], device_id=(mate, r), device_id_type=MESH)

    def rs_step(name, k):
        if k > 0:
            rs_copy(name, k - 1).wait_recv()
        if name == "dz":
            if k == 1:
                for c in range(2):
                    add_blocks(c, phz[0].at[c], tiles)
            if k == 2:
                for q in range(tiles):
                    total = stage[0, q].astype(F32) + phz[1][q].astype(F32)
                    gdown[q * rb : (q + 1) * rb, pl.ds(aligned(half * r), half)] = total
        elif name[0] == "d":
            if k > 0:
                add_blocks(chunk_of(name), phd[k - 1].at[int(name[1])], sections >> k)
        elif k > 0:
            at = others.index(name)
            if k < bits:
                add_blocks(tiles + at, pho[k - 1].at[at], sections >> k)
            else:
                view = final_view(name)
                view[...] = stage[tiles + at, 0].astype(F32) + pho[k - 1][at, 0].astype(F32)
        if k < phases_of(name):
            rs_copy(name, k).start()
        elif name == "dz" or name[0] != "d":
            final_copy(name).start()

    def final_view(name):
        if name == "dz":
            return gdown.at[:, pl.ds(aligned(half * r), half)]
        out = {"u": gup, "o": gwout, "q": gqkv}[name[0]]
        c = int(name[1]) if len(name) > 1 else 0
        return out.at[:, pl.ds(aligned(c * width + half * r), half)]

    def final_copy(name):
        at = parts.index(name)
        return pltpu.make_async_remote_copy(
            final_view(name), final_view(name), f_send.at[at], f_recv.at[at], device_id=core, device_id_type=MESH)

    plan = PLAN if bits == 4 else later_plan(parts, phases_of)

    def at(point):
        for item in plan.get(point, ()):
            name, k = item.split(".")
            if name == "g":
                gain_step(int(k))
                continue
            if k == "0" and name != "dz":
                core_copy(name).wait()
                add_blocks(chunk_of(name), own_v.at[slot_of[name]], sections)
            rs_step(name, int(k))

    def gain_copy(k):
        mate = mates[k]
        return pltpu.make_async_remote_copy(
            gs.at[k], gr.at[k], gain_sem.at[0, k], gain_sem.at[1, k], device_id=mate, device_id_type=MESH)

    def gain_step(k):
        if k > 0:
            gain_copy(k - 1).wait_recv()
            gs[k] = gs[k - 1] + gr[k - 1]
        if k <= bits:
            gain_copy(k).start()
        else:
            gout[...] = gs[k]

    def do_copy(p):
        return pltpu.make_async_remote_copy(
            do_own.at[:, pl.ds(aligned(half * (1 - r)), half)], do_v.at[p, pl.ds(aligned(tokens * r, 16), tokens), :],
            do_sem.at[0, p], do_sem.at[1, p], device_id=core, device_id_type=MESH)

    def ds_copy(p, pair, sending):
        at = r if sending else 1 - r
        cols = pl.ds(aligned(half * at + PAIR * pair), PAIR)
        return pltpu.make_async_remote_copy(
            ds_tmp.at[pair, :, 1 - r], ds_v.at[:, pl.ds(p * tokens, tokens), cols], ds_send.at[p, pair],
            ds_recv.at[p, pair], device_id=core, device_id_type=MESH)

    def attention_pair(p, pair):
        off = aligned(pair * PAIR)
        cols = pl.ds(off, PAIR)
        blocks_of = [slice(i * tokens, (i + 1) * tokens) for i in range(2)]
        queries, grads = [], []
        for rows in blocks_of:
            q = qkv_v[p, 0, rows, cols]
            g = do_v[p, rows, cols]
            queries.append([q * mask for mask in masks])
            grads.append([g * mask for mask in masks])
        dq = [None, None]
        for src in range(p + 1):
            for j in range(2):
                at = blocks_of[j]
                key = qkv_v[src, 1, at, cols]
                value = qkv_v[src, 2, at, cols]
                keys = jnp.concatenate([key * mask for mask in masks], axis=0)
                probs, d_scores = [], []
                for i in range(j, 2):
                    for h in range(2):
                        lse = lse_v[p, 2 * pair + h, :, blocks_of[i]]
                        dd = dd_v[2 * pair + h, :, blocks_of[i]]
                        prob = jnp.exp(dot_nt(key, queries[i][h]) + bias[i + j].astype(F32) - lse)
                        d_prob = dot_nt(value, grads[i][h])
                        d_scores.append(low(prob * (d_prob - dd)))
                        probs.append(low(prob))
                    term = dot_tn(jnp.concatenate(d_scores[-2:], axis=0), keys)
                    dq[i] = term if dq[i] is None else dq[i] + term
                q_all = jnp.concatenate([v for i in range(j, 2) for v in queries[i]], axis=0)
                g_all = jnp.concatenate([v for i in range(j, 2) for v in grads[i]], axis=0)
                d_key = dot(jnp.concatenate(d_scores, axis=1), q_all)
                d_value = dot(jnp.concatenate(probs, axis=1), g_all)
                for kv, term in enumerate((d_key, d_value)):
                    if p == 1 and src == 0:
                        dkv0[kv, at, cols] = term.astype(dkv0.dtype)
                    else:
                        ds_tmp[pair, 1 + kv, j] = low(term if p == 1 else term + dkv0[kv, at, cols].astype(F32))
        for i in range(2):
            ds_tmp[pair, 0, i] = low(dq[i] * (HEAD ** -0.5))
        mine = pl.ds(aligned(half * r + off), PAIR)
        for c in range(3):
            ds_v[c, pl.ds(p * tokens, tokens), mine] = ds_tmp[pair, c, r]
        ds_copy(p, pair, True).start()

    def sg_own_copy():
        return pltpu.make_async_copy(dm_v, sgrad.at[0, m], sg_local.at[0])

    head_row = lax.broadcasted_iota(jnp.int32, (16, half), 0)
    head_of = lax.broadcasted_iota(jnp.int32, (16, half), 1)
    picks = low(jnp.where((head_of >= head_row * HEAD) & (head_of < (head_row + 1) * HEAD), 1.0, 0.0))

    own_pass.wait()
    other_pass.wait()

    for p in (1, 0):
        if p == 0:
            def join(rows):
                total = df_v[0, rows, :].astype(F32) + low(dm_v[rows, :]).astype(F32)
                dn_v[rows, :] = total
                df_v[0, rows, :] = low(total)

            by_rows(tokens, join)
            ld_gp0.wait()
            ld_g.wait()
            at("join")
            for t in range(tiles):
                put_tile(f"d{t}", lambda at, n: g_v[:, :, t * width + at : t * width + at + n].reshape(2 * tokens, n),
                         df_v[...].reshape(2 * tokens, width))
                at(f"wd{t}")
        for t, cols in enumerate(blocks):
            if p == 1:
                ld_first[t][0].wait()
                ld_first[t][1].wait()
            dg = dot_nt(df_v[p], wdown_v[cols, :])
            du_v[p, :, cols] = low(dg * du_v[p, :, cols].astype(F32))
        if p == 1:
            ld_up.wait()
            ld_m1.wait()
            ld_out = load(wout, wout_v, 6)
            ld_qkv = load(qkv_i, qkv_v, 7)
            ld_o32 = load(o32_i.at[1], o32_v, 8)
            ld_lse = load(lse_i, lse_v, 9)
        else:
            ld_o = load(o_i, df_v, 15)
            ld_m0.wait()

            @pl.when(m == 1)
            def _():
                sg_own_copy().wait()

            at("units")
            ld_b.wait()
            for t in range(tiles):
                put_tile(f"u{t}", lambda at, n: b_v[:, :, at : at + n].reshape(2 * tokens, n),
                         du_v[:, :, t * width : (t + 1) * width].reshape(2 * tokens, width))
                at(f"wu{t}")
            ld_a = load(a_i, b_v, 16)
        dm_v[...] = dot_nt(du_v[p], wup_v[...])
        if p == 0:
            at("db")

        def norm_two_back(rows):
            xh, scale = norm_parts(m_v[rows, :])
            dy = dm_v[rows, :]
            gs[0, 1:2, :] += jnp.sum(dy * xh, axis=0, keepdims=True)
            dxh = dy * gain2
            dv = scale * (dxh - mean_of(dxh) - xh * mean_of(dxh * xh))
            grad = df_v[1, rows, :].astype(F32) if p == 1 else dn_v[rows, :]
            total = grad + dv
            dm_v[rows, :] = total
            dc_v[p, rows, :] = low(total)

        by_rows(tokens, norm_two_back)
        ld_x = load(x_i.at[p], m_v, 11 + p)
        if p == 1:
            ld_out.wait()
            ld_wqkv = load(wqkv, wqkv_v, 10)
        else:
            at("ln2")
            do_copy(1).wait_send()
        do_own[...] = low(dot_nt(dc_v[p], wout_v[...]))
        do_copy(p).start()
        do_v[p, pl.ds(aligned(tokens * r, 16), tokens), :] = do_own[:, pl.ds(aligned(half * r), half)]
        if p == 1:
            ld_qkv.wait()
            ld_lse.wait()
            ld_o32.wait()
            ld_gp0 = load(gp_i.at[0], du_v.at[0], 18)
            hid_own.wait()
            hid_out = pltpu.make_async_copy(sg_send_v, hidden.at[0, m], in_sem.at[5])
            hid_out.start()
            ld_g = load(g_i, g_v, 13)
            ld_b = load(b_i, b_v, 14)
        else:
            at("do")
            ld_o320.wait()
        do_copy(p).wait_recv()
        for i in range(2):
            rows = slice(i * tokens, (i + 1) * tokens)
            prod = do_v[p, rows, :].astype(F32) * o32_v[rows, :]
            upper = low(prod)
            rest = low(prod - upper.astype(F32))
            sums = dot_nt(picks, upper) + dot_nt(picks, rest)
            for h in range(2 * pairs):
                dd_v[h, :, rows] = sums[h : h + 1, :]
        if p == 1:
            ld_o320 = load(o32_i.at[0], o32_v, 20)

            def pair_step(pair, carry):
                attention_pair(1, pair)
                return carry

            lax.fori_loop(0, pairs, pair_step, 0)
        else:
            at("dowait")
            for pair in range(pairs):
                ds_copy(1, pair, True).wait_send()
            for pair in range(pairs):
                attention_pair(0, pair)
                at(f"at{pair}")
            ld_o.wait()
            put_tile("o", lambda at, n: df_v[:, :, at : at + n].reshape(2 * tokens, n), dc_v[...].reshape(2 * tokens, width))
            at("wo")
            ld_a.wait()
        for pair in range(pairs):
            ds_copy(p, pair, False).wait_recv()
        if p == 1:
            ld_wqkv.wait()
        else:
            at("dswait")
            for c in range(3):
                put_tile(f"q{c}", lambda at, n: b_v[:, :, at : at + n].reshape(2 * tokens, n), ds_v[c])
                at(f"wq{c}")
        ld_x.wait()
        for c in range(3):
            term = dot_nt(ds_v[c, p * tokens : (p + 1) * tokens, :], wqkv_v[:, c * width : (c + 1) * width])
            dn_v[...] = term if c == 0 else dn_v[...] + term
        if p == 0:
            at("da")

        def norm_one_back(rows):
            xh, scale = norm_parts(m_v[rows, :])
            dy = dn_v[rows, :]
            gs[0, 0:1, :] += jnp.sum(dy * xh, axis=0, keepdims=True)
            dxh = dy * gain1
            dv = scale * (dxh - mean_of(dxh) - xh * mean_of(dxh * xh))
            dm_v[rows, :] = dm_v[rows, :] + dv

        by_rows(tokens, norm_one_back)

        if p == 1:
            hid_out.wait()

        @pl.when(m == p)
        def _():
            sg_own_copy().start()

        @pl.when(m != p)
        def _():
            sg_send_v[...] = low(dm_v[...])
            pltpu.make_async_remote_copy(
                sg_send_v, sg_recv_v, sg_sem.at[0], sg_sem.at[1], device_id=relay, device_id_type=MESH).start()

        if p == 1:
            ld_m0 = load(m_i.at[0], m_v, 19)

    gain_step(0)
    at("ln1")
    at("end")
    sg_copy = pltpu.make_async_remote_copy(
        sg_send_v, sg_recv_v, sg_sem.at[0], sg_sem.at[1], device_id=relay, device_id_type=MESH)
    sg_copy.wait_recv()
    dn_v[...] = sg_recv_v[...].astype(F32)
    sg_last = pltpu.make_async_copy(dn_v, sgrad.at[0, 1 - m], sg_local.at[1])
    sg_last.start()

    for name in parts:
        if name == "dz" or name[0] != "d":
            final_copy(name).wait()
        for k in range(phases_of(name)):
            rs_copy(name, k).wait_send()
    hid_copy.wait()
    for k in range(bits + 1):
        gain_copy(k).wait_send()
    do_copy(0).wait_send()
    for pair in range(pairs):
        ds_copy(0, pair, True).wait_send()
    sg_copy.wait_send()

    @pl.when(m == 0)
    def _():
        sg_own_copy().wait()

    sg_last.wait()


def shape(dims, dtype):
    return jax.ShapeDtypeStruct(dims, dtype)


def forward_call(stream, cot, seg, gains, weights):
    wqkv, wout, wup, wdown = weights
    _, _, tokens, width = stream.shape
    units = wup.shape[1]
    half = width // 2
    length = 2 * tokens
    pairs = half // PAIR
    saved = [
        shape((2, tokens, width), F32),
        shape((2, tokens, width), BF16),
        shape((2, 3, length, half), BF16),
        shape((2, length, half), F32),
        shape((2, tokens, width), BF16),
        shape((2, tokens, width), F32),
        shape((2, tokens, width), BF16),
        shape((2, tokens, units), BF16),
        shape((2, tokens, units), BF16),
        shape((2, 2 * pairs, 1, length), F32),
    ]
    anyspace = pl.BlockSpec(memory_space=pl.ANY)
    vmem = pl.BlockSpec(memory_space=pltpu.VMEM)
    V = pltpu.VMEM
    sem = pltpu.SemaphoreType.DMA
    return pl.pallas_call(
        forward_kernel,
        out_shape=[shape((2, tokens, width), BF16), shape((tokens, width), BF16)] + saved,
        in_specs=[anyspace, anyspace, vmem, vmem, vmem] + [anyspace] * 4,
        out_specs=[anyspace] * 12,
        scratch_shapes=[
            V(wqkv.shape, BF16), V(wout.shape, BF16), V(wup.shape, BF16), V(wdown.shape, BF16),
            V((tokens, width), BF16), V((tokens, width), BF16), V((2, tokens, width), F32),
            V((2, tokens, width), BF16), V((2, 3, tokens, width), BF16), V((2, 3, length, half), BF16),
            V((2, length, half), F32), V((2, pairs, 2, tokens, PAIR), BF16), V((2, tokens, width), BF16),
            V((2, tokens, width), F32), V((2, tokens, width), BF16), V((2, tokens, units), BF16),
            V((2, tokens, units), BF16), V((tokens, width), F32), V((2, tokens, width), BF16),
            V((2, 2 * pairs, 1, length), F32), V((3, tokens, tokens), F32),
            sem((5,)), sem((2 * (9 + 2 * (units // width)),)), sem((2, 2)), sem((2,)),
            sem((2, 3)), sem((2, 3)), sem((2, pairs)), sem((2, pairs)),
        ],
        compiler_params=pltpu.CompilerParams(collective_id=0, has_side_effects=True, vmem_limit_bytes=VMEM_LIMIT),
        name="forward",
    )(stream, cot, seg, *gains, wqkv, wout, wup, wdown)


def backward_call(hid, cot, cotx, seg, gains, weights, saved, sections):
    wqkv, wout, wup, wdown = weights
    _, _, tokens, width = cot.shape
    units = wup.shape[1]
    half = width // 2
    length = 2 * tokens
    pairs = half // PAIR
    tiles = units // width
    chunks = 2 * tiles + 4
    bits = sections.bit_length() - 1
    assert 2 ** bits == sections and bits >= 4 and tiles == 4
    rb = width // sections
    spare = F32 if rb % 16 == 0 else BF16
    anyspace = pl.BlockSpec(memory_space=pl.ANY)
    vmem = pl.BlockSpec(memory_space=pltpu.VMEM)
    V = pltpu.VMEM
    sem = pltpu.SemaphoreType.DMA

    def body(*refs):
        fixed = len(scratch) + 20 + 7
        phd, refs_z = refs[fixed : fixed + bits - 2], refs[fixed + bits - 2 :]
        phz, pho, rest = refs_z[:2], refs_z[2 : 2 + bits], refs_z[2 + bits :]
        backward_kernel(bits, *refs[:fixed], phd, phz, pho, *rest)

    scratch = [
        V(wqkv.shape, BF16), V(wout.shape, BF16), V(wup.shape, BF16), V(wdown.shape, BF16),
        V((tokens, width), F32), V((length, half), F32),
        V((2, 3, length, half), BF16), V((2, 2 * pairs, 1, length), F32),
        V((2, tokens, width), BF16), V((2, tokens, units), BF16),
        V((2, tokens, width), BF16), V((2, tokens, units), BF16), V((2, tokens, width), BF16),
        V((3, 2 * tokens, width), BF16), V((tokens, width), BF16), V((2, length, half), BF16),
        V((2 * pairs, 1, length), F32), V((tokens, width), F32), V((tokens, width), F32),
        V((3, tokens, tokens), spare), V((2, length, half), spare),
        V((pairs, 3, 2, tokens, PAIR), BF16),
        V((tokens, width), BF16), V((tokens, width), BF16),
        V((width // 2, width), F32), V((tiles, sections, rb, half), BF16), V((tiles, sections, rb, half), BF16),
        V((chunks, sections, rb, half), BF16),
    ]
    ph = [V((tiles, sections >> (k + 1), rb, half), BF16) for k in range(bits - 2)]
    ph += [V((2, tiles, rb, half), BF16), V((tiles, rb, half), BF16)]
    ph += [V((chunks - tiles, sections >> (k + 1), rb, half), BF16) for k in range(bits)]
    rest = [
        V((bits + 2, 8, width), F32), V((bits + 1, 8, width), F32),
        sem((21 + 2 * tiles,)), sem((2,)), sem((2,)), sem((2,)), sem((2, 2)), sem((2, pairs)), sem((2, pairs)),
        sem((chunks + 1,)), sem((chunks + 1,)), sem((chunks + 1, bits)), sem((chunks + 1, bits)),
        sem((chunks + 1,)), sem((chunks + 1,)), sem((2, bits + 1)),
    ]
    return pl.pallas_call(
        body,
        out_shape=[
            shape(cot.shape, BF16), shape(cot.shape, F32), shape((8, width), F32), shape((rb, 3 * width), F32), shape((rb, width), F32),
            shape((rb, units), F32), shape((tiles * rb, width), F32),
        ],
        in_specs=[anyspace, anyspace, anyspace, vmem, vmem, vmem] + [anyspace] * 14,
        out_specs=[anyspace] * 2 + [vmem] * 5,
        scratch_shapes=scratch + ph + rest,
        compiler_params=pltpu.CompilerParams(collective_id=1, has_side_effects=True, vmem_limit_bytes=VMEM_LIMIT),
        name="backward",
    )(hid, cot, cotx, seg, *gains, wqkv, wout, wup, wdown, *saved)


def finish_kernel(sections, gout, *refs):
    n = (len(refs) - 3) // 3
    sources, targets, gain1, gain2 = refs[:n], refs[n : 2 * n], refs[2 * n], refs[2 * n + 1]
    held, sem = refs[2 * n + 2 : -1], refs[-1]
    ins = [pltpu.make_async_copy(a, b, sem.at[0, i]) for i, (a, b) in enumerate(zip(sources, held))]
    outs = [pltpu.make_async_copy(a, b, sem.at[1, i]) for i, (a, b) in enumerate(zip(held, targets))]
    for copy in ins:
        copy.start()
    width = gout.shape[1]
    rb = width // sections
    s = lax.axis_index("section")
    turned = pltpu.roll(gout[...], lax.rem(width - s * rb, width), 1)
    gain1[...] = turned[0, :rb]
    gain2[...] = turned[1, :rb]
    for arrived, copy in zip(ins, outs):
        arrived.wait()
        copy.start()
    for copy in outs:
        copy.wait()


def finish_call(gout, arrays, sections):
    anyspace = pl.BlockSpec(memory_space=pl.ANY)
    vmem = pl.BlockSpec(memory_space=pltpu.VMEM)
    gain = shape((gout.shape[1] // sections,), F32)
    return pl.pallas_call(
        functools.partial(finish_kernel, sections),
        out_shape=[shape(a.shape, a.dtype) for a in arrays] + [gain, gain],
        in_specs=[vmem] + [anyspace] * len(arrays),
        out_specs=[anyspace] * len(arrays) + [vmem, vmem],
        scratch_shapes=[pltpu.VMEM(a.shape, a.dtype) for a in arrays] + [pltpu.SemaphoreType.DMA((2, len(arrays)))],
        compiler_params=pltpu.CompilerParams(vmem_limit_bytes=VMEM_LIMIT),
        name="finish",
    )(gout, *arrays)


def per_device(stream, segment_ids, ln1_gain, w_qkv, w_out, ln2_gain, w_up, w_down, cotangent):
    sections = lax.axis_size("section")
    gains = (ln1_gain, ln2_gain)
    weights = (w_qkv, w_out, w_up, w_down)
    hid, cotx, *saved = forward_call(stream, cotangent, segment_ids, gains, weights)
    hidden, sgrad, gout, gqkv, gwout, gup, gdown = backward_call(hid, cotangent, cotx, segment_ids, gains, weights, saved, sections)
    hidden, sgrad, gqkv, gwout, gup, gdown, gain1, gain2 = finish_call(
        gout, (hidden, sgrad, gqkv, gwout, gup, gdown), sections)
    return (hidden, sgrad, gain1, gqkv, gwout, gain2, gup, gdown)


def solution(mesh):
    rows = P("section", None, "rows", None)
    assert mesh.shape["rows"] == 2
    return jax.shard_map(
        per_device,
        mesh=mesh,
        in_specs=(rows, P("section", None, None), P(), P(), P(), P(), P(), P(), rows),
        out_specs=(rows, rows, P("section"), P("section", None), P("section", None), P("section"),
                   P("section", None), P("section", None)),
        check_vma=False,
    )
```
